512 devices in a mesh: dp: 8 (over x, core), expert: 64 (over z, y).
Axes of the slice: x: 4, y: 4, z: 16, core: 2. Of those that a mesh axis runs over, the one named last changes fastest.
Arguments:
- tokens: bfloat16 [2048, 4096], P('expert', 'dp'), may hold values from -6 to 6
- grad_out: bfloat16 [2048, 4096], P('expert', 'dp'), may hold values from -6 to 6
- route_prob: float32 [2048, 8], P('expert'), may hold values from 0.05 to 0.5
- expert_ids: int32 [2048, 8], P('expert'), may hold values from 0 to 63, all different within a row; in each aligned block of 32 rows (0 to 31, 32 to 63, ...) at most 5 rows name the same one
- w_gate: bfloat16 [64, 1536, 4096], P('expert', 'dp'), may hold values from -0.09375 to 0.09375
- w_up: bfloat16 [64, 1536, 4096], P('expert', 'dp'), may hold values from -0.09375 to 0.09375
- w_down: bfloat16 [64, 1536, 4096], P('expert', 'dp'), may hold values from -0.15625 to 0.15625
- adapter_a: bfloat16 [64, 64, 1536], P('expert', None, 'dp'), may hold values from -0.15625 to 0.15625
- adapter_b: bfloat16 [64, 64, 4096], P('expert', None, 'dp'), may hold values from -0.09375 to 0.09375
Outputs:
- grad_tokens: bfloat16 [2048, 4096], P('expert', 'dp')
- grad_adapter_a: float32 [64, 64, 1536], P('expert', None, 'dp')
- grad_adapter_b: float32 [64, 64, 4096], P('expert', None, 'dp')
The draws below stay inside these ranges and needn't reach their ends.
Inputs may be any that keep to these rules, and one draw needn't show every extreme that they name: `expert_ids`: each row names 8 different experts. In each aligned block of 32 tokens (those of one index of the expert axis) no expert is named by more than 5 rows, a bound that some block reaches.
All inputs are finite; a program needn't handle non-finite values.
Results may differ from the reference program's by a relative error of at most 0.019.
Values may be sent and summed in bfloat16 or wider, within the bound.
No kernel may reach another device: no remote copies, remote signals or barrier semaphores. Data moves between devices by JAX's collectives and lax.ppermute only.
A program may use at most 64 MiB of HBM per device.

```python
import math
import jax
import jax.numpy as jnp
import numpy as np
from jax import lax

D = 4096
FF = 1536
RANK = 64
TOP = 8
TOK_E = 32
EXPERTS = 64
TOKENS = 2048
CAP = 5
N_DP = 8
N_EXPERT = 64


def block_levels(key, extent, pieces, smallest, high):
    def one(axis_at, shards_of):
        steps = jax.random.uniform(jax.random.fold_in(jax.random.fold_in(key, 6), axis_at), (shards_of,), jnp.float32, smallest / len(pieces), high / len(pieces))
        return jnp.repeat(jnp.exp(steps), extent[axis_at] // shards_of).reshape((-1,) + (1,) * (len(extent) - axis_at - 1))

    level = one(*pieces[0])
    for cut in pieces[1:]:
        level = level * one(*cut)
    return level


def shared_out(own_key, own, number, rows, amount, top, limit, slope):
    sequence = jax.random.permutation(own_key, amount)
    packed, usual = shares(amount, rows * top, limit, slope, True), shares(amount, rows * top, limit, slope, False)
    places = jnp.arange(amount)

    def named(lengths, turn):
        used = int((lengths > 0).sum())
        fixed = max(1, used // 4)
        passed = fixed + (places - fixed + turn * (used - fixed)) % max(1, amount - fixed)
        return jnp.zeros((amount,), jnp.int32).at[sequence[jnp.where(places < fixed, places, passed)]].set(jnp.asarray(lengths, jnp.int32))

    lengths = jnp.where(number % 4 == 0, named(packed, number // 4), named(usual, number - number // 4 - 1))
    mixed = jax.random.permutation(jax.random.fold_in(own, 3), amount)
    source_of, receiver = mixed[0:amount // 2 * 2:2], mixed[1:amount // 2 * 2:2]
    margin = jnp.minimum(lengths[source_of] - 1, limit - lengths[receiver]) // 2
    margin = jnp.where((source_of == sequence[0]) | (receiver == sequence[0]) | (lengths[receiver] == 0), 0, jnp.maximum(margin, 0))
    passed = jax.random.randint(jax.random.fold_in(own, 4), (amount // 2,), 0, 1 << 20) % (margin + 1)
    lengths = lengths.at[source_of].add(-passed).at[receiver].add(passed)
    labels = jnp.searchsorted(jnp.cumsum(lengths), jnp.arange(rows * top), side="right").astype(jnp.int32)
    grid = labels.reshape(top, rows).T
    grid = grid[jax.random.permutation(jax.random.fold_in(own, 1), rows)]
    turn = jax.random.randint(jax.random.fold_in(own, 2), (rows, 1), 0, top)
    return jnp.take_along_axis(grid, (jnp.arange(top)[None, :] + turn) % top, axis=1)


def shares(count, total, bound, slope, full):
    loads = [(1 << 20) // math.isqrt(standing ** slope) + 1 for standing in range(1, count + 1)]
    largest = bound if full else min(bound, max(-(-total // count), total * loads[0] // sum(loads)))
    least = 1 if total - largest >= count - 1 else 0
    holding, surplus = [largest] + [least] * (count - 1), total - largest - least * (count - 1)
    while surplus > 0:
        movable = [i for i in range(1, count) if holding[i] < largest] or [i for i in range(1, count) if holding[i] < bound]
        whole, left = sum([loads[i] for i in movable]), surplus
        for i in movable:
            addition = min(bound - holding[i], max(1, left * loads[i] // whole), surplus)
            holding[i] = holding[i] + addition
            surplus = surplus - addition
    return np.array(holding)


def centred(own_key, extent, spread, most, cuts=(), held_as=jnp.bfloat16):
    result = spread * jax.random.normal(own_key, extent, jnp.float32)
    if cuts:
        result = result * block_levels(own_key, extent, cuts, -0.22, 0.18)
    return jnp.clip(result, -most, most).astype(held_as)


def setup_inputs(seed: int = 0) -> dict:
    streams_of = jax.random.split(jax.random.key(seed), 10)
    tokens = centred(streams_of[0], (TOKENS, D), 1.0, 6.0, ((0, 64), (1, 8)))
    grad_out = centred(streams_of[1], (TOKENS, D), 1.0, 6.0, ((0, 64), (1, 8)))
    route_prob = jnp.clip(0.05 + 0.45 * jax.random.uniform(streams_of[2], (TOKENS, TOP), jnp.float32) ** block_levels(streams_of[2], (TOKENS, TOP), ((0, 64),), -0.2, 0.2), 0.05, 0.5)
    expert_ids_keys = jax.random.split(jax.random.fold_in(streams_of[3], 1), TOKENS // TOK_E)
    expert_ids_turns = jax.random.permutation(jax.random.fold_in(streams_of[3], 3), TOKENS // TOK_E)
    expert_ids = jax.vmap(lambda own, number: shared_out(jax.random.fold_in(streams_of[3], 2), own, number, TOK_E, EXPERTS, TOP, CAP, 2))(expert_ids_keys, expert_ids_turns).reshape((TOKENS, TOP))
    w_gate = centred(streams_of[4], (EXPERTS, FF, D), D ** -0.5, 0.09375, ((0, 64), (1, 8)))
    w_up = centred(streams_of[5], (EXPERTS, FF, D), D ** -0.5, 0.09375, ((0, 64), (1, 8)))
    w_down = centred(streams_of[6], (EXPERTS, FF, D), FF ** -0.5, 0.15625, ((0, 64), (1, 8)))
    adapter_a = centred(streams_of[7], (EXPERTS, RANK, FF), FF ** -0.5, 0.15625, ((0, 64), (2, 8)))
    adapter_b = centred(streams_of[8], (EXPERTS, RANK, D), D ** -0.5, 0.09375, ((0, 64), (2, 8)))
    return dict(tokens=tokens, grad_out=grad_out, route_prob=route_prob, expert_ids=expert_ids, w_gate=w_gate, w_up=w_up, w_down=w_down, adapter_a=adapter_a, adapter_b=adapter_b)


def contract(left, right, left_dim, right_dim):
    return lax.dot_general(left, right, (((left_dim,), (right_dim,)), ((), ())), preferred_element_type=jnp.float32)


def expert_backward(x_rows, scaled, gate_mat, up_mat, down_mat, low_a, low_b):
    gate_pre = contract(x_rows, gate_mat, 1, 1)
    up_pre = contract(x_rows, up_mat, 1, 1)
    sigma = jax.nn.sigmoid(gate_pre)
    active = gate_pre * sigma
    hidden = (active * up_pre).astype(jnp.bfloat16)
    low_u = contract(scaled, low_b, 1, 1).astype(jnp.bfloat16)
    grad_hidden = contract(scaled, down_mat, 1, 1) + jnp.dot(low_u, low_a, preferred_element_type=jnp.float32)
    low_v = contract(hidden, low_a, 1, 1).astype(jnp.bfloat16)
    grad_gate = (grad_hidden * up_pre * sigma * (1.0 + gate_pre * (1.0 - sigma))).astype(jnp.bfloat16)
    grad_up = (grad_hidden * active).astype(jnp.bfloat16)
    grad_a = contract(low_u, hidden, 0, 0)
    grad_b = contract(low_v, scaled, 0, 0)
    width_block = FF // N_DP
    route_grad = jnp.zeros((x_rows.shape[0], D), jnp.float32)
    for block_idx in range(N_DP):
        lower = block_idx * width_block
        upper = lower + width_block
        term = contract(grad_gate[:, lower:upper], gate_mat[lower:upper, :], 1, 0)
        term = term + contract(grad_up[:, lower:upper], up_mat[lower:upper, :], 1, 0)
        rounded = lax.optimization_barrier(term.astype(jnp.bfloat16))
        route_grad = route_grad + rounded.astype(jnp.float32)
    return route_grad, grad_a, grad_b


def reference(tokens, grad_out, route_prob, expert_ids, w_gate, w_up, w_down, adapter_a, adapter_b):
    row_limit = N_EXPERT * CAP

    def per_expert(total, inputs):
        expert_idx, gate_mat, up_mat, down_mat, low_a, low_b = inputs
        hit = expert_ids == expert_idx
        routed = jnp.sum(hit.astype(jnp.int32), axis=1)
        weight_all = jnp.sum(jnp.where(hit, route_prob, jnp.zeros_like(route_prob)), axis=1)
        picked = jnp.nonzero(routed, size=row_limit, fill_value=0)[0].astype(jnp.int32)
        live = jnp.arange(row_limit, dtype=jnp.int32) < jnp.sum(routed)
        weight_rows = jnp.where(live, weight_all[picked], jnp.zeros((row_limit,), weight_all.dtype))
        x_rows = tokens[picked]
        scaled = (weight_rows[:, None] * grad_out[picked].astype(jnp.float32)).astype(jnp.bfloat16)
        route_grad, grad_a, grad_b = expert_backward(x_rows, scaled, gate_mat, up_mat, down_mat, low_a, low_b)
        total = total.at[picked].add(route_grad)
        return total, (grad_a, grad_b)

    start = jnp.zeros((TOKENS, D), jnp.float32)
    experts_all = jnp.arange(EXPERTS, dtype=jnp.int32)
    total, grads = lax.scan(per_expert, start, (experts_all, w_gate, w_up, w_down, adapter_a, adapter_b))
    return total.astype(jnp.bfloat16), grads[0], grads[1]
```

```python
import functools

import jax
import jax.numpy as jnp
from jax import lax
from jax.experimental import pallas as pl
from jax.experimental.pallas import tpu as pltpu
from jax.sharding import Mesh, PartitionSpec as P

CAP = 5
BF = jnp.bfloat16
F32 = jnp.float32
PARAMS = pltpu.CompilerParams(vmem_limit_bytes=48 * 1024 * 1024)


def nt(left, right):
    return lax.dot_general(left, right, (((1,), (1,)), ((), ())), preferred_element_type=F32)


def tn(left, right):
    return lax.dot_general(left, right, (((0,), (0,)), ((), ())), preferred_element_type=F32)


def nn(left, right):
    return jnp.dot(left, right, preferred_element_type=F32)


def pack_kernel(ids_ref, prob_ref, tok_ref, dy_ref, x_ref, s_ref, code_ref):
    experts, width = code_ref.shape[0], tok_ref.shape[1]
    count = ids_ref.shape[1]
    own = lax.broadcasted_iota(jnp.int32, (experts, count), 0)
    hit = jnp.zeros((experts, count), F32)
    weight = jnp.zeros((experts, count), F32)
    for k in range(ids_ref.shape[0]):
        same = ids_ref[k : k + 1, :] == own
        hit = jnp.where(same, 1.0, hit)
        weight = jnp.where(same, prob_ref[k : k + 1, :], weight)
    first = lax.broadcasted_iota(jnp.int32, (count, count), 0)
    second = lax.broadcasted_iota(jnp.int32, (count, count), 1)
    before = jnp.where(first < second, 1.0, 0.0).astype(BF)
    slot = nn(hit.astype(BF), before)
    code = jnp.where(hit > 0.5, slot, -1.0)
    code_ref[...] = code
    for s in range(CAP):
        mine = code == float(s)
        pick = jnp.where(mine, 1.0, 0.0).astype(BF)
        scale = jnp.sum(jnp.where(mine, weight, 0.0), axis=1, keepdims=True)
        cols = slice(s * width, (s + 1) * width)
        x_ref[:, cols] = nn(pick, tok_ref[...]).astype(BF)
        s_ref[:, cols] = (nn(pick, dy_ref[...]) * scale).astype(BF)


def rows_of(block, width):
    return jnp.concatenate([block[:, s * width : (s + 1) * width] for s in range(CAP)], axis=0)


def gate_kernel(core_ref, own_ref, other_ref, wg_ref, wu_ref, a_ref, gate_ref, up_ref, hid_ref, v_ref):
    chips, experts, wide = own_ref.shape
    width = wide // CAP
    core = core_ref[0]
    gate = jnp.zeros(gate_ref.shape, F32)
    up = jnp.zeros(up_ref.shape, F32)
    for ref, which in ((own_ref, core), (other_ref, 1 - core)):
        for x in range(chips):
            rows = rows_of(ref[x], width)
            cols = pl.ds(pl.multiple_of((2 * x + which) * width, width), width)
            gate += nt(rows, wg_ref[:, cols])
            up += nt(rows, wu_ref[:, cols])
    gate_ref[...] = gate
    up_ref[...] = up
    hidden = (gate * jax.nn.sigmoid(gate) * up).astype(BF)
    hid_ref[...] = hidden
    v_ref[...] = nt(hidden, a_ref[...]).astype(BF)


def grad_kernel(
    core_ref, own_ref, other_ref, gate_ref, up_ref, hid_ref, v_ref, wg_ref, wu_ref, wd_ref, a_ref,
    keep_ref, send_ref, ga_ref,
):
    chips, experts = own_ref.shape[:2]
    width = wd_ref.shape[1] // (2 * chips)
    rank = a_ref.shape[0]
    core = core_ref[0]
    grad = jnp.zeros(gate_ref.shape, F32)
    low = jnp.zeros((experts * CAP, rank), F32)
    for ref, which in ((own_ref, core), (other_ref, 1 - core)):
        for x in range(chips):
            block = ref[x]
            rows = rows_of(block, width)
            cols = pl.ds(pl.multiple_of((2 * x + which) * width, width), width)
            grad += nt(rows, wd_ref[:, cols])
            low += nt(rows, block[:, CAP * width :])
    low_u = low.astype(BF)
    grad += nn(low_u, a_ref[...])
    ga_ref[...] = tn(low_u, hid_ref[...])
    gate = gate_ref[...]
    sigma = jax.nn.sigmoid(gate)
    grad_gate = (grad * up_ref[...] * sigma * (1.0 + gate * (1.0 - sigma))).astype(BF)
    grad_up = (grad * (gate * sigma)).astype(BF)
    for ref, which in ((keep_ref, core), (send_ref, 1 - core)):
        for x in range(chips):
            cols = pl.ds(pl.multiple_of((2 * x + which) * width, width), width)
            term = (nn(grad_gate, wg_ref[:, cols]) + nn(grad_up, wu_ref[:, cols])).astype(BF)
            for s in range(CAP):
                ref[x, :, s * width : (s + 1) * width] = term[s * experts : (s + 1) * experts]
            for s in range(CAP):
                ref[x, :, CAP * width + s * rank : CAP * width + (s + 1) * rank] = v_ref[
                    s * experts : (s + 1) * experts
                ]


def pair_kernel(a_ref, b_ref, o_ref):
    o_ref[...] = (a_ref[...].astype(F32) + b_ref[...].astype(F32)).astype(BF)


def total_kernel(in_ref, out_ref, v_ref):
    total = in_ref[0].astype(F32)
    for x in range(1, in_ref.shape[0]):
        total += in_ref[x].astype(F32)
    low = total.astype(BF)
    wide = out_ref.shape[1]
    experts, rank = out_ref.shape[0], v_ref.shape[1]
    out_ref[...] = low[:, :wide]
    for s in range(CAP):
        v_ref[s * experts : (s + 1) * experts] = low[:, wide + s * rank : wide + (s + 1) * rank]


def adapter_kernel(v_ref, s_ref, o_ref):
    o_ref[...] = tn(v_ref[...], rows_of(s_ref[...], o_ref.shape[1]))


def combine_kernel(code_ref, r_ref, o_ref):
    width = o_ref.shape[1]
    total = jnp.zeros(o_ref.shape, F32)
    for s in range(CAP):
        pick = jnp.where(code_ref[...] == float(s), 1.0, 0.0).astype(BF)
        total += tn(pick, r_ref[:, s * width : (s + 1) * width])
    o_ref[...] = total.astype(BF)


def call(body, outs, *args, scalars=0):
    vmem = pl.BlockSpec(memory_space=pltpu.VMEM)
    smem = pl.BlockSpec(memory_space=pltpu.SMEM)
    return pl.pallas_call(
        body,
        out_shape=outs,
        in_specs=[smem] * scalars + [vmem] * (len(args) - scalars),
        out_specs=jax.tree.map(lambda _: vmem, outs),
        compiler_params=PARAMS,
    )(*args)


def per_device(tokens, grad_out, prob, ids, w_gate, w_up, w_down, adapter_a, adapter_b):
    experts = lax.axis_size(("z", "y"))
    chips = lax.axis_size("x")
    width = tokens.shape[1]
    wide = CAP * width
    rank = adapter_b.shape[1]
    sds = jax.ShapeDtypeStruct
    core = lax.axis_index("c").reshape(1).astype(jnp.int32)
    swap = [(0, 1), (1, 0)]

    def route(block):
        return lax.all_to_all(block, ("z", "y"), 0, 0, tiled=True)

    def spread(block):
        own = lax.all_to_all(jnp.broadcast_to(block[None], (chips,) + block.shape), "x", 0, 0, tiled=True)
        return own, lax.ppermute(own, "c", swap)

    x_pack, s_pack, code = call(
        pack_kernel,
        (sds((experts, wide), BF), sds((experts, wide), BF), sds((experts, tokens.shape[0]), F32)),
        ids.T, prob.T, tokens, grad_out,
    )
    x_in = route(x_pack)
    s_in = route(s_pack)
    x_own, x_other = spread(x_in)
    s_own, s_other = spread(jnp.concatenate([s_in, adapter_b[0]], axis=1))
    hidden_units = w_gate.shape[1]
    routes = experts * CAP
    gate, up, hidden, part_v = call(
        gate_kernel,
        (
            sds((routes, hidden_units), F32), sds((routes, hidden_units), F32),
            sds((routes, hidden_units), BF), sds((routes, rank), BF),
        ),
        core, x_own, x_other, w_gate[0], w_up[0], adapter_a[0], scalars=1,
    )
    full = wide + CAP * rank
    keep, send, grad_a = call(
        grad_kernel,
        (sds((chips, experts, full), BF), sds((chips, experts, full), BF), sds((rank, hidden_units), F32)),
        core, s_own, s_other, gate, up, hidden, part_v, w_gate[0], w_up[0], w_down[0], adapter_a[0],
        scalars=1,
    )
    got = lax.ppermute(send, "c", swap)
    pair = call(pair_kernel, sds((chips, experts, full), BF), keep, got)
    quad = lax.all_to_all(pair, "x", 0, 0, tiled=True)
    total, low_v = call(total_kernel, (sds((experts, wide), BF), sds((routes, rank), BF)), quad)
    back = route(total)
    grad_b = call(adapter_kernel, sds((rank, width), F32), low_v, s_in)
    out = call(combine_kernel, sds(tokens.shape, BF), code, back)
    return out, grad_a[None], grad_b[None]


def solution(mesh):
    fine = Mesh(mesh.devices.reshape(4, 2, 16, 4), ("x", "c", "z", "y"))
    dp, ex = ("x", "c"), ("z", "y")
    specs = (
        P(ex, dp), P(ex, dp), P(ex, None), P(ex, None),
        P(ex, dp, None), P(ex, dp, None), P(ex, dp, None), P(ex, None, dp), P(ex, None, dp),
    )
    return jax.shard_map(
        per_device,
        mesh=fine,
        in_specs=specs,
        out_specs=(P(ex, dp), P(ex, None, dp), P(ex, None, dp)),
        check_vma=False,
    )
```

```python
import jax
import jax.numpy as jnp
from jax import lax
from jax.experimental import pallas as pl
from jax.experimental.pallas import tpu as pltpu
from jax.sharding import Mesh, PartitionSpec as P

CAP = 5
BF = jnp.bfloat16
F32 = jnp.float32
PARAMS = pltpu.CompilerParams(vmem_limit_bytes=16 * 1024 * 1024)


def nt(left, right):
    return lax.dot_general(left, right, (((1,), (1,)), ((), ())), preferred_element_type=F32)


def tn(left, right):
    return lax.dot_general(left, right, (((0,), (0,)), ((), ())), preferred_element_type=F32)


def nn(left, right):
    return jnp.dot(left, right, preferred_element_type=F32)


def lanes(index, width):
    return pl.ds(pl.multiple_of(index * width, width), width)


def pack_kernel(ids_ref, prob_ref, tok_ref, dy_ref, out_ref, code_ref):
    experts, width = code_ref.shape[0], tok_ref.shape[1]
    count = ids_ref.shape[1]
    own = lax.broadcasted_iota(jnp.int32, (experts, count), 0)
    hit = jnp.zeros((experts, count), F32)
    weight = jnp.zeros((experts, count), F32)
    for k in range(ids_ref.shape[0]):
        same = ids_ref[k : k + 1, :] == own
        hit = jnp.where(same, 1.0, hit)
        weight = jnp.where(same, prob_ref[k : k + 1, :], weight)
    first = lax.broadcasted_iota(jnp.int32, (count, count), 0)
    second = lax.broadcasted_iota(jnp.int32, (count, count), 1)
    before = jnp.where(first < second, 1.0, 0.0).astype(BF)
    slot = nn(hit.astype(BF), before)
    code = jnp.where(hit > 0.5, slot, -1.0)
    code_ref[...] = code
    for s in range(CAP):
        mine = code == float(s)
        pick = jnp.where(mine, 1.0, 0.0).astype(BF)
        scale = jnp.sum(jnp.where(mine, weight, 0.0), axis=1, keepdims=True)
        base = 2 * s * width
        out_ref[:, base : base + width] = nn(pick, tok_ref[...]).astype(BF)
        out_ref[:, base + width : base + 2 * width] = (nn(pick, dy_ref[...]) * scale).astype(BF)


def split_kernel(in_ref, x_ref, s_ref):
    experts = in_ref.shape[0]
    width = s_ref.shape[1]
    for s in range(CAP):
        rows = slice(s * experts, (s + 1) * experts)
        base = 2 * s * width
        block = in_ref[:, base : base + width]
        for x in range(x_ref.shape[0]):
            x_ref[x, rows] = block
        s_ref[rows] = in_ref[:, base + width : base + 2 * width]


def prep_kernel(me_ref, wg_ref, wu_ref, wd_ref, swap_ref, d1_ref, d2_ref, d3_ref):
    chip, core = me_ref[0], me_ref[1]
    chips, units, width = swap_ref.shape[1:]
    for x in range(chips):
        cols = lanes(2 * x + 1 - core, width)
        swap_ref[0, x] = wg_ref[:, cols]
        swap_ref[1, x] = wu_ref[:, cols]
    for d, ref in ((1, d1_ref), (2, d2_ref), (3, d3_ref)):
        ref[...] = wd_ref[:, lanes(lax.rem(chip + d, chips), 2 * width)]


def part_kernel(me_ref, s_ref, t_ref, wd_ref, d1_ref, d2_ref, d3_ref, b_ref, o_ref, out_ref):
    chip, core = me_ref[0], me_ref[1]
    chips = out_ref.shape[0]
    units = wd_ref.shape[0]
    width = s_ref.shape[1]
    mine, other = s_ref[...], t_ref[...]
    low = (nt(mine, b_ref[...]) + nt(other, o_ref[...])).astype(BF)
    for d, ref in ((0, None), (1, d1_ref), (2, d2_ref), (3, d3_ref)):
        if ref is None:
            w_mine = wd_ref[:, lanes(2 * chip + core, width)]
            w_other = wd_ref[:, lanes(2 * chip + 1 - core, width)]
        else:
            w_mine = ref[:, lanes(core, width)]
            w_other = ref[:, lanes(1 - core, width)]
        to = lax.rem(chip + chips - d, chips)
        out_ref[to, :, :units] = (nt(mine, w_mine) + nt(other, w_other)).astype(BF)
        out_ref[to, :, units:] = low


def gate_kernel(me_ref, x_ref, wg_ref, wu_ref, swap_ref, keep_ref, send_ref):
    core = me_ref[1]
    chips, routes, width = x_ref.shape
    units = wg_ref.shape[0]
    keep = [jnp.zeros((routes, units), F32)] * 2
    send = [jnp.zeros((routes, units), F32)] * 2
    for x in range(chips):
        rows = x_ref[x]
        cols = lanes(2 * x + core, width)
        for i, ref in enumerate((wg_ref, wu_ref)):
            keep[i] = keep[i] + nt(rows, ref[:, cols])
            send[i] = send[i] + nt(rows, swap_ref[i, x])
    for i in range(2):
        keep_ref[i] = keep[i]
        send_ref[i] = send[i].astype(BF)


def act_kernel(keep_ref, got_ref, a_ref, gate_ref, up_ref, hid_ref, v_ref):
    gate = keep_ref[0] + got_ref[0].astype(F32)
    up = keep_ref[1] + got_ref[1].astype(F32)
    gate_ref[...] = gate
    up_ref[...] = up
    hidden = (gate * jax.nn.sigmoid(gate) * up).astype(BF)
    hid_ref[...] = hidden
    v_ref[...] = nt(hidden, a_ref[...]).astype(BF)


def grad_kernel(in_ref, gate_ref, up_ref, hid_ref, a_ref, out_ref, ga_ref):
    units = gate_ref.shape[1]
    total = in_ref[0].astype(F32)
    for x in range(1, in_ref.shape[0]):
        total += in_ref[x].astype(F32)
    low_u = total[:, units:].astype(BF)
    grad = total[:, :units] + nn(low_u, a_ref[...])
    ga_ref[...] = tn(low_u, hid_ref[...])
    gate = gate_ref[...]
    sigma = jax.nn.sigmoid(gate)
    out_ref[0] = (grad * up_ref[...] * sigma * (1.0 + gate * (1.0 - sigma))).astype(BF)
    out_ref[1] = (grad * (gate * sigma)).astype(BF)


def back_kernel(me_ref, g_ref, h_ref, wg_ref, wu_ref, swap_ref, out_ref):
    core = me_ref[1]
    chips, _, width = out_ref.shape
    for x in range(chips):
        cols = lanes(2 * x + core, width)
        term = nn(g_ref[0], wg_ref[:, cols]) + nn(g_ref[1], wu_ref[:, cols])
        term += nn(h_ref[0], swap_ref[0, x]) + nn(h_ref[1], swap_ref[1, x])
        out_ref[x] = term.astype(BF)


def total_kernel(in_ref, out_ref):
    experts = out_ref.shape[0]
    width = in_ref.shape[2]
    for s in range(CAP):
        rows = slice(s * experts, (s + 1) * experts)
        total = in_ref[0, rows].astype(F32)
        for x in range(1, in_ref.shape[0]):
            total += in_ref[x, rows].astype(F32)
        out_ref[:, s * width : (s + 1) * width] = total.astype(BF)


def pair_kernel(a_ref, b_ref, o_ref):
    o_ref[...] = (a_ref[...].astype(F32) + b_ref[...].astype(F32)).astype(BF)


def adapter_kernel(v0_ref, v1_ref, v2_ref, v3_ref, s_ref, o_ref):
    low = v0_ref[...].astype(F32) + v1_ref[...].astype(F32)
    low += v2_ref[...].astype(F32) + v3_ref[...].astype(F32)
    o_ref[...] = tn(low.astype(BF), s_ref[...])


def combine_kernel(code_ref, r_ref, o_ref):
    width = o_ref.shape[1]
    total = jnp.zeros(o_ref.shape, F32)
    for s in range(CAP):
        pick = jnp.where(code_ref[...] == float(s), 1.0, 0.0).astype(BF)
        total += tn(pick, r_ref[:, s * width : (s + 1) * width])
    o_ref[...] = total.astype(BF)


def call(body, outs, *args, scalars=0):
    vmem = pl.BlockSpec(memory_space=pltpu.VMEM)
    smem = pl.BlockSpec(memory_space=pltpu.SMEM)
    return pl.pallas_call(
        body,
        out_shape=outs,
        in_specs=[smem] * scalars + [vmem] * (len(args) - scalars),
        out_specs=jax.tree.map(lambda _: vmem, outs),
        compiler_params=PARAMS,
    )(*args)


def per_device(tokens, grad_out, prob, ids, w_gate, w_up, w_down, adapter_a, adapter_b):
    experts = lax.axis_size(("z", "y"))
    chips = lax.axis_size("x")
    count, width = tokens.shape
    rank = adapter_b.shape[1]
    units = w_gate.shape[1]
    routes = experts * CAP
    w_gate, w_up, w_down, adapter_a, adapter_b = (
        w_gate[0], w_up[0], w_down[0], adapter_a[0], adapter_b[0],
    )
    sds = jax.ShapeDtypeStruct
    me = jnp.stack([lax.axis_index("x"), lax.axis_index("c")]).astype(jnp.int32)

    def swap(block):
        return lax.ppermute(block, "c", [(0, 1), (1, 0)])

    def shift(block, by):
        return lax.ppermute(block, "x", [(i, (i + by) % chips) for i in range(chips)])

    def over_x(block):
        return lax.all_to_all(block, "x", 0, 0, tiled=True)

    def route(block):
        return lax.all_to_all(block, ("z", "y"), 0, 0, tiled=True)

    packed, code = call(
        pack_kernel,
        (sds((experts, 2 * CAP * width), BF), sds((experts, count), F32)),
        ids.T, prob.T, tokens, grad_out,
    )
    arrived = route(packed)

    half, *down = call(
        prep_kernel,
        (sds((2, chips, units, width), BF),) + (sds((units, 2 * width), BF),) * 3,
        me, w_gate, w_up, w_down, scalars=1,
    )
    half = swap(half)
    down = [shift(block, d + 1) for d, block in enumerate(down)]
    b_other = swap(adapter_b)
    arrived, half, b_other, *down = lax.optimization_barrier((arrived, half, b_other, *down))

    x_four, s_own = call(split_kernel, (sds((chips, routes, width), BF), sds((routes, width), BF)), arrived)
    x_all = over_x(x_four)
    s_other = swap(s_own)
    part = call(
        part_kernel, sds((chips, routes, units + rank), BF),
        me, s_own, s_other, w_down, *down, adapter_b, b_other, scalars=1,
    )
    parts = over_x(part)
    keep, send = call(
        gate_kernel,
        (sds((2, routes, units), F32), sds((2, routes, units), BF)),
        me, x_all, w_gate, w_up, half, scalars=1,
    )
    got = swap(send)
    gate, up, hidden, v_own = call(
        act_kernel,
        (sds((routes, units), F32),) * 2 + (sds((routes, units), BF), sds((routes, rank), BF)),
        keep, got, adapter_a,
    )
    grads, grad_a = call(
        grad_kernel,
        (sds((2, routes, units), BF), sds((rank, units), F32)),
        parts, gate, up, hidden, adapter_a,
    )
    grads_other = swap(grads)
    back = call(
        back_kernel, sds((chips, routes, width), BF),
        me, grads, grads_other, w_gate, w_up, half, scalars=1,
    )
    backs = over_x(back)
    total = call(total_kernel, sds((experts, CAP * width), BF), backs)
    home = route(total)

    v_pair = call(pair_kernel, sds((routes, rank), BF), v_own, swap(v_own))
    v_all = [v_pair] + [shift(v_pair, d) for d in (1, 2, 3)]
    grad_b = call(adapter_kernel, sds((rank, width), F32), *v_all, s_own)
    out = call(combine_kernel, sds(tokens.shape, BF), code, home)
    return out, grad_a[None], grad_b[None]


def solution(mesh):
    fine = Mesh(mesh.devices.reshape(4, 2, 16, 4), ("x", "c", "z", "y"))
    dp, ex = ("x", "c"), ("z", "y")
    specs = (
        P(ex, dp), P(ex, dp), P(ex, None), P(ex, None),
        P(ex, dp, None), P(ex, dp, None), P(ex, dp, None), P(ex, None, dp), P(ex, None, dp),
    )
    return jax.shard_map(
        per_device,
        mesh=fine,
        in_specs=specs,
        out_specs=(P(ex, dp), P(ex, None, dp), P(ex, None, dp)),
        check_vma=False,
    )
```

```python
import jax
import jax.numpy as jnp
from jax import lax
from jax.experimental import pallas as pl
from jax.experimental.pallas import tpu as pltpu
from jax.sharding import Mesh, PartitionSpec as P

CAP = 5
BF = jnp.bfloat16
F32 = jnp.float32
LANE = 128
PARAMS = pltpu.CompilerParams(vmem_limit_bytes=16 * 1024 * 1024)


def nt(left, right):
    return lax.dot_general(left, right, (((1,), (1,)), ((), ())), preferred_element_type=F32)


def tn(left, right):
    return lax.dot_general(left, right, (((0,), (0,)), ((), ())), preferred_element_type=F32)


def nn(left, right):
    return jnp.dot(left, right, preferred_element_type=F32)


def lanes(index, width):
    return pl.ds(pl.multiple_of(index * width, width), width)


def fetch(pairs, sems):
    copies = [pltpu.make_async_copy(src, dst, sems.at[i]) for i, (src, dst) in enumerate(pairs)]
    for copy in copies:
        copy.start()
    for copy in copies:
        copy.wait()


def pack_kernel(ids_hbm, prob_hbm, tok_hbm, dy_hbm, out_ref, ids_ref, prob_ref, tok_ref, dy_ref, sems):
    fetch(
        [(ids_hbm, ids_ref), (prob_hbm, prob_ref), (tok_hbm, tok_ref), (dy_hbm, dy_ref)], sems
    )
    rows = out_ref.shape[0]
    count, width = tok_ref.shape
    parts = 2 * width // LANE
    span = parts * count
    row = lax.broadcasted_iota(jnp.int32, (rows, span), 0)
    lane = lax.broadcasted_iota(jnp.int32, (rows, span), 1)
    own = jnp.where(lax.rem(row, parts) == lax.div(lane, count), lax.div(row, parts), -1)
    ids = jnp.concatenate([ids_ref[...]] * parts, axis=1)
    prob = jnp.concatenate([prob_ref[...]] * parts, axis=1)
    hit = jnp.zeros((rows, span), F32)
    weight = jnp.zeros((rows, span), F32)
    for k in range(ids.shape[0]):
        same = ids[k : k + 1, :] == own
        hit = jnp.where(same, 1.0, hit)
        weight = jnp.where(same, prob[k : k + 1, :], weight)
    weight = jnp.where(lax.rem(row, parts) < parts // 2, hit, weight)
    first = lax.broadcasted_iota(jnp.int32, (span, span), 0)
    second = lax.broadcasted_iota(jnp.int32, (span, span), 1)
    near = lax.div(first, count) == lax.div(second, count)
    before = jnp.where(near & (first < second), 1.0, 0.0).astype(BF)
    slot = nn(hit.astype(BF), before)
    code = jnp.where(hit > 0.5, slot, -1.0)
    table = jnp.concatenate(
        [ref[:, c : c + LANE] for ref in (tok_ref, dy_ref) for c in range(0, width, LANE)], axis=0
    )
    for s in range(CAP):
        mine = code == float(s)
        pick = jnp.where(mine, 1.0, 0.0).astype(BF)
        scale = jnp.sum(jnp.where(mine, weight, 0.0), axis=1, keepdims=True)
        out_ref[:, s * LANE : (s + 1) * LANE] = (nn(pick, table) * scale).astype(BF)


def code_of(ids, experts):
    count = ids.shape[1]
    own = lax.broadcasted_iota(jnp.int32, (experts, count), 0)
    hit = jnp.zeros((experts, count), F32)
    for k in range(ids.shape[0]):
        hit = jnp.where(ids[k : k + 1, :] == own, 1.0, hit)
    first = lax.broadcasted_iota(jnp.int32, (count, count), 0)
    second = lax.broadcasted_iota(jnp.int32, (count, count), 1)
    before = jnp.where(first < second, 1.0, 0.0).astype(BF)
    return jnp.where(hit > 0.5, nn(hit.astype(BF), before), -1.0)


def split_kernel(in_ref, x_hbm, s_hbm, x_ref, s_ref, sems):
    total = in_ref.shape[0]
    width = s_ref.shape[1]
    parts = 2 * width // LANE
    experts = total // parts
    first = lax.broadcasted_iota(jnp.int32, (total, total), 0)
    second = lax.broadcasted_iota(jnp.int32, (total, total), 1)
    there = lax.rem(first, experts) * parts + lax.div(first, experts)
    perm = jnp.where(second == there, 1.0, 0.0).astype(BF)
    rows = nn(perm, in_ref[...]).astype(BF)
    for r in range(parts):
        ref = x_ref if r < parts // 2 else s_ref
        at = (r % (parts // 2)) * LANE
        for s in range(CAP):
            ref[s * experts : (s + 1) * experts, at : at + LANE] = rows[
                r * experts : (r + 1) * experts, s * LANE : (s + 1) * LANE
            ]
    chips = x_hbm.shape[0]
    fetch([(x_ref, x_hbm.at[x]) for x in range(chips)] + [(s_ref, s_hbm)], sems)


def prep_kernel(me_ref, wg_ref, wu_ref, wd_ref, swap_ref, d0_ref, d1_ref, d2_ref, d3_ref):
    chip, core = me_ref[0], me_ref[1]
    chips, units, width = swap_ref.shape[1:]
    for x in range(chips):
        cols = lanes(2 * x + 1 - core, width)
        swap_ref[0, x] = wg_ref[:, cols]
        swap_ref[1, x] = wu_ref[:, cols]
    for d, ref in enumerate((d0_ref, d1_ref, d2_ref, d3_ref)):
        ref[...] = wd_ref[:, lanes(lax.rem(chip + d, chips), 2 * width)]


def part_kernel(me_ref, *refs):
    core = me_ref[1]
    sources, outs, held, sems = refs[:8], refs[8:12], refs[12:20], refs[20]
    fetch(list(zip(sources, held)), sems)
    s_ref, t_ref, b_ref, o_ref = held[:4]
    units, width = held[4].shape[0], s_ref.shape[1]
    mine, other = s_ref[...], t_ref[...]
    low = (nt(mine, b_ref[...]) + nt(other, o_ref[...])).astype(BF)
    for ref, out in zip(held[4:], outs):
        w_mine, w_other = ref[:, lanes(core, width)], ref[:, lanes(1 - core, width)]
        out[:, :units] = (nt(mine, w_mine) + nt(other, w_other)).astype(BF)
        out[:, units:] = low


def gate_kernel(me_ref, x_ref, wg_ref, wu_ref, swap_ref, *refs):
    keep_ref, send_ref = refs[-2:]
    core = me_ref[1]
    chips, routes, width = x_ref.shape
    units = wg_ref.shape[0]
    keep = [jnp.zeros((routes, units), F32)] * 2
    send = [jnp.zeros((routes, units), F32)] * 2
    for x in range(chips):
        rows = x_ref[x]
        cols = lanes(2 * x + core, width)
        for i, ref in enumerate((wg_ref, wu_ref)):
            keep[i] = keep[i] + nt(rows, ref[:, cols])
            send[i] = send[i] + nt(rows, swap_ref[i, x])
    for i in range(2):
        keep_ref[i] = keep[i]
        send_ref[i] = send[i].astype(BF)


def grad_kernel(keep_ref, got_ref, p0_ref, p1_ref, p2_ref, p3_ref, a_ref, out_ref, ga_ref, v_ref):
    units = keep_ref.shape[2]
    gate = keep_ref[0] + got_ref[0].astype(F32)
    up = keep_ref[1] + got_ref[1].astype(F32)
    sigma = jax.nn.sigmoid(gate)
    active = gate * sigma
    hidden = (active * up).astype(BF)
    v_ref[...] = nt(hidden, a_ref[...]).astype(BF)
    total = p0_ref[...].astype(F32) + p1_ref[...].astype(F32)
    total += p2_ref[...].astype(F32) + p3_ref[...].astype(F32)
    low_u = total[:, units:].astype(BF)
    grad = total[:, :units] + nn(low_u, a_ref[...])
    ga_ref[...] = tn(low_u, hidden)
    out_ref[0] = (grad * up * sigma * (1.0 + gate * (1.0 - sigma))).astype(BF)
    out_ref[1] = (grad * active).astype(BF)


def back_kernel(me_ref, g_ref, h_ref, wg_ref, wu_ref, swap_ref, out_ref):
    core = me_ref[1]
    chips, _, width = out_ref.shape
    for x in range(chips):
        cols = lanes(2 * x + core, width)
        term = nn(g_ref[0], wg_ref[:, cols]) + nn(g_ref[1], wu_ref[:, cols])
        term += nn(h_ref[0], swap_ref[0, x]) + nn(h_ref[1], swap_ref[1, x])
        out_ref[x] = term.astype(BF)


def total_kernel(in_ref, out_ref):
    experts = out_ref.shape[0]
    width = in_ref.shape[2]
    for s in range(CAP):
        rows = slice(s * experts, (s + 1) * experts)
        total = in_ref[0, rows].astype(F32)
        for x in range(1, in_ref.shape[0]):
            total += in_ref[x, rows].astype(F32)
        out_ref[:, s * width : (s + 1) * width] = total.astype(BF)


def pair_kernel(a_ref, b_ref, o_ref):
    o_ref[...] = (a_ref[...].astype(F32) + b_ref[...].astype(F32)).astype(BF)


def adapter_kernel(ids_ref, v0_ref, v1_ref, v2_ref, v3_ref, s_ref, o_ref, code_ref):
    code_ref[...] = code_of(ids_ref[...], code_ref.shape[0])
    low = v0_ref[...].astype(F32) + v1_ref[...].astype(F32)
    low += v2_ref[...].astype(F32) + v3_ref[...].astype(F32)
    o_ref[...] = tn(low.astype(BF), s_ref[...])


def combine_kernel(code_ref, r_ref, o_ref):
    width = o_ref.shape[1]
    total = jnp.zeros(o_ref.shape, F32)
    for s in range(CAP):
        pick = jnp.where(code_ref[...] == float(s), 1.0, 0.0).astype(BF)
        total += tn(pick, r_ref[:, s * width : (s + 1) * width])
    o_ref[...] = total.astype(BF)


def call(body, outs, *args, scalars=0, places=(), ends=(), scratch=()):
    vmem = pl.BlockSpec(memory_space=pltpu.VMEM)
    smem = pl.BlockSpec(memory_space=pltpu.SMEM)
    places = places or [vmem] * (len(args) - scalars)
    return pl.pallas_call(
        body,
        out_shape=outs,
        in_specs=[smem] * scalars + list(places),
        out_specs=ends or jax.tree.map(lambda _: vmem, outs),
        scratch_shapes=list(scratch),
        compiler_params=PARAMS,
    )(*args)


def per_device(tokens, grad_out, prob, ids, w_gate, w_up, w_down, adapter_a, adapter_b):
    experts = lax.axis_size(("z", "y"))
    chips = lax.axis_size("x")
    count, width = tokens.shape
    rank = adapter_b.shape[1]
    units = w_gate.shape[1]
    routes = experts * CAP
    w_gate, w_up, w_down, adapter_a, adapter_b = (
        w_gate[0], w_up[0], w_down[0], adapter_a[0], adapter_b[0],
    )
    sds = jax.ShapeDtypeStruct
    me = jnp.stack([lax.axis_index("x"), lax.axis_index("c")]).astype(jnp.int32)

    def swap(block):
        return lax.ppermute(block, "c", [(0, 1), (1, 0)])

    def shift(block, by):
        return lax.ppermute(block, "x", [(i, (i + by) % chips) for i in range(chips)])

    def over_x(block):
        return lax.all_to_all(block, "x", 0, 0, tiled=True)

    def route(block):
        return lax.all_to_all(block, ("z", "y"), 0, 0, tiled=True)

    parts = 2 * width // LANE
    slow = pl.BlockSpec(memory_space=pltpu.HBM)

    def pin(*arrays):
        return [pltpu.with_memory_space_constraint(x, pltpu.HBM) for x in arrays]

    near = pl.BlockSpec(memory_space=pltpu.VMEM)
    far = pl.BlockSpec(memory_space=pltpu.HBM)
    dma = pltpu.SemaphoreType.DMA

    packed = call(
        pack_kernel, sds((experts * parts, CAP * LANE), BF),
        *pin(ids.T, prob.T, tokens, grad_out),
        places=[slow] * 4,
        scratch=[
            pltpu.VMEM(ids.T.shape, ids.dtype), pltpu.VMEM(prob.T.shape, F32),
            pltpu.VMEM(tokens.shape, BF), pltpu.VMEM(tokens.shape, BF), dma((4,)),
        ],
    )
    arrived = route(packed.reshape(experts, parts, CAP * LANE))

    half, *down = call(
        prep_kernel,
        (sds((2, chips, units, width), BF),) + (sds((units, 2 * width), BF),) * 4,
        me, w_gate, w_up, w_down, scalars=1,
    )
    half = swap(half)
    down = down[:1] + [shift(block, d + 1) for d, block in enumerate(down[1:])]
    b_other = swap(adapter_b)
    arrived, half, b_other, *down = lax.optimization_barrier((arrived, half, b_other, *down))

    x_four, s_own = call(
        split_kernel, (pltpu.HBM((chips, routes, width), BF), pltpu.HBM((routes, width), BF)),
        arrived.reshape(experts * parts, CAP * LANE),
        ends=(far, far),
        scratch=[pltpu.VMEM((routes, width), BF)] * 2 + [dma((chips + 1,))],
    )
    x_all = over_x(x_four)
    s_other = swap(s_own)
    share = sds((routes, units + rank), BF)
    sources = (s_own, s_other, adapter_b, b_other, *down)
    part, *sent = call(
        part_kernel, (share,) * chips, me, *pin(*sources), scalars=1, places=[slow] * len(sources),
        scratch=[pltpu.VMEM(x.shape, BF) for x in sources] + [dma((len(sources),))],
    )
    sent = [shift(block, chips - 1 - d) for d, block in enumerate(sent)]
    keep, send = call(
        gate_kernel,
        (sds((2, routes, units), F32), sds((2, routes, units), BF)),
        me, x_all, w_gate, w_up, half, *sent, scalars=1,
        places=[near] * 4 + [pl.BlockSpec(memory_space=pl.ANY)] * len(sent),
    )
    got = swap(send)
    grads, grad_a, v_own = call(
        grad_kernel,
        (sds((2, routes, units), BF), sds((rank, units), F32), sds((routes, rank), BF)),
        keep, got, part, *sent, adapter_a,
    )
    grads_other = swap(grads)
    back = call(
        back_kernel, sds((chips, routes, width), BF),
        me, grads, grads_other, w_gate, w_up, half, scalars=1,
    )
    backs = over_x(back)
    total = call(total_kernel, sds((experts, CAP * width), BF), backs)
    home = route(total.reshape(experts, 2, CAP * width // 2)).reshape(experts, CAP * width)

    v_pair = call(pair_kernel, sds((routes, rank), BF), v_own, swap(v_own))
    v_all = [v_pair] + [shift(v_pair, d) for d in (1, 2, 3)]
    grad_b, code = call(
        adapter_kernel, (sds((rank, width), F32), sds((experts, count), F32)), ids.T, *v_all, s_own
    )
    out = call(combine_kernel, sds(tokens.shape, BF), code, home)
    return out, grad_a[None], grad_b[None]


def solution(mesh):
    fine = Mesh(mesh.devices.reshape(4, 2, 16, 4), ("x", "c", "z", "y"))
    dp, ex = ("x", "c"), ("z", "y")
    specs = (
        P(ex, dp), P(ex, dp), P(ex, None), P(ex, None),
        P(ex, dp, None), P(ex, dp, None), P(ex, dp, None), P(ex, None, dp), P(ex, None, dp),
    )
    return jax.shard_map(
        per_device,
        mesh=fine,
        in_specs=specs,
        out_specs=(P(ex, dp), P(ex, None, dp), P(ex, None, dp)),
        check_vma=False,
    )
```

```python
import jax
import jax.numpy as jnp
from jax import lax
from jax.experimental import pallas as pl
from jax.experimental.pallas import tpu as pltpu
from jax.sharding import Mesh, PartitionSpec as P

CAP = 5
BF = jnp.bfloat16
F32 = jnp.float32
LANE = 128
PARAMS = pltpu.CompilerParams(vmem_limit_bytes=16 * 1024 * 1024)


def nt(left, right):
    return lax.dot_general(left, right, (((1,), (1,)), ((), ())), preferred_element_type=F32)


def tn(left, right):
    return lax.dot_general(left, right, (((0,), (0,)), ((), ())), preferred_element_type=F32)


def nn(left, right):
    return jnp.dot(left, right, preferred_element_type=F32)


def lanes(index, width):
    return pl.ds(pl.multiple_of(index * width, width), width)


def fetch(pairs, sems):
    copies = [pltpu.make_async_copy(src, dst, sems.at[i]) for i, (src, dst) in enumerate(pairs)]
    for copy in copies:
        copy.start()
    for copy in copies:
        copy.wait()


def pack_kernel(ids_hbm, prob_hbm, tok_hbm, dy_hbm, out_ref, ids_ref, prob_ref, tok_ref, dy_ref, sems):
    fetch(
        [(ids_hbm, ids_ref), (prob_hbm, prob_ref), (tok_hbm, tok_ref), (dy_hbm, dy_ref)], sems
    )
    rows = out_ref.shape[0]
    count, width = tok_ref.shape
    parts = 2 * width // LANE
    span = parts * count
    row = lax.broadcasted_iota(jnp.int32, (rows, span), 0)
    lane = lax.broadcasted_iota(jnp.int32, (rows, span), 1)
    own = jnp.where(lax.rem(row, parts) == lax.div(lane, count), lax.div(row, parts), -1)
    ids = jnp.concatenate([ids_ref[...]] * parts, axis=1)
    prob = jnp.concatenate([prob_ref[...]] * parts, axis=1)
    hit = jnp.zeros((rows, span), F32)
    weight = jnp.zeros((rows, span), F32)
    for k in range(ids.shape[0]):
        same = ids[k : k + 1, :] == own
        hit = jnp.where(same, 1.0, hit)
        weight = jnp.where(same, prob[k : k + 1, :], weight)
    weight = jnp.where(lax.rem(row, parts) < parts // 2, hit, weight)
    first = lax.broadcasted_iota(jnp.int32, (span, span), 0)
    second = lax.broadcasted_iota(jnp.int32, (span, span), 1)
    near = lax.div(first, count) == lax.div(second, count)
    before = jnp.where(near & (first < second), 1.0, 0.0).astype(BF)
    slot = nn(hit.astype(BF), before)
    code = jnp.where(hit > 0.5, slot, -1.0)
    table = jnp.concatenate(
        [ref[:, c : c + LANE] for ref in (tok_ref, dy_ref) for c in range(0, width, LANE)], axis=0
    )
    for s in range(CAP):
        mine = code == float(s)
        pick = jnp.where(mine, 1.0, 0.0).astype(BF)
        scale = jnp.sum(jnp.where(mine, weight, 0.0), axis=1, keepdims=True)
        out_ref[:, s * LANE : (s + 1) * LANE] = (nn(pick, table) * scale).astype(BF)


def code_of(ids, experts):
    count = ids.shape[1]
    own = lax.broadcasted_iota(jnp.int32, (experts, count), 0)
    hit = jnp.zeros((experts, count), F32)
    for k in range(ids.shape[0]):
        hit = jnp.where(ids[k : k + 1, :] == own, 1.0, hit)
    first = lax.broadcasted_iota(jnp.int32, (count, count), 0)
    second = lax.broadcasted_iota(jnp.int32, (count, count), 1)
    before = jnp.where(first < second, 1.0, 0.0).astype(BF)
    return jnp.where(hit > 0.5, nn(hit.astype(BF), before), -1.0)


def split_kernel(in_ref, x_hbm, s_hbm, x_ref, s_ref, sems):
    total = in_ref.shape[0]
    width = s_ref.shape[1]
    parts = 2 * width // LANE
    experts = total // parts
    first = lax.broadcasted_iota(jnp.int32, (total, total), 0)
    second = lax.broadcasted_iota(jnp.int32, (total, total), 1)
    there = lax.rem(first, experts) * parts + lax.div(first, experts)
    perm = jnp.where(second == there, 1.0, 0.0).astype(BF)
    rows = nn(perm, in_ref[...]).astype(BF)
    for r in range(parts):
        ref = x_ref if r < parts // 2 else s_ref
        at = (r % (parts // 2)) * LANE
        for s in range(CAP):
            ref[s * experts : (s + 1) * experts, at : at + LANE] = rows[
                r * experts : (r + 1) * experts, s * LANE : (s + 1) * LANE
            ]
    chips = x_hbm.shape[0]
    fetch([(x_ref, x_hbm.at[x]) for x in range(chips)] + [(s_ref, s_hbm)], sems)


def prep_kernel(me_ref, wg_ref, wu_ref, wd_ref, swap_ref, d0_ref, d1_ref, d2_ref, d3_ref):
    chip, core = me_ref[0], me_ref[1]
    chips, units, width = swap_ref.shape[1:]
    for x in range(chips):
        cols = lanes(2 * x + 1 - core, width)
        swap_ref[0, x] = wg_ref[:, cols]
        swap_ref[1, x] = wu_ref[:, cols]
    for d, ref in enumerate((d0_ref, d1_ref, d2_ref, d3_ref)):
        ref[...] = wd_ref[:, lanes(lax.rem(chip + d, chips), 2 * width)]


def part_kernel(me_ref, *refs):
    chip, core = me_ref[0], me_ref[1]
    sources, out_hbm, held, out_ref, sems = refs[:8], refs[8], refs[9:17], refs[17], refs[18]
    fetch(list(zip(sources, held)), sems)
    s_ref, t_ref, b_ref, o_ref = held[:4]
    units, width = held[4].shape[0], s_ref.shape[1]
    chips = out_ref.shape[0]
    mine, other = s_ref[...], t_ref[...]
    low = (nt(mine, b_ref[...]) + nt(other, o_ref[...])).astype(BF)
    for d, ref in enumerate(held[4:]):
        w_mine, w_other = ref[:, lanes(core, width)], ref[:, lanes(1 - core, width)]
        to = lax.rem(chip + chips - d, chips)
        out_ref[to, :, :units] = (nt(mine, w_mine) + nt(other, w_other)).astype(BF)
        out_ref[to, :, units:] = low
    fetch([(out_ref, out_hbm)], sems)


def gate_kernel(
    me_ref, x_hbm, wg_hbm, wu_hbm, half_hbm, keep_hbm, send_ref,
    x_ref, w_ref, half_ref, keep_ref, sems, sem,
):
    core = me_ref[1]
    chips, routes, width = x_ref.shape
    units = w_ref.shape[2]
    copies = []
    for x in range(chips):
        cols = lanes(2 * x + core, width)
        pairs = [
            (x_hbm.at[x], x_ref.at[x]), (wg_hbm.at[:, cols], w_ref.at[0, x]),
            (wu_hbm.at[:, cols], w_ref.at[1, x]), (half_hbm.at[:, x], half_ref.at[:, x]),
        ]
        copies.append([pltpu.make_async_copy(p, q, sems.at[x, i]) for i, (p, q) in enumerate(pairs)])
        for copy in copies[x]:
            copy.start()
    keep = [jnp.zeros((routes, units), F32)] * 2
    send = [jnp.zeros((routes, units), F32)] * 2
    for x in range(chips):
        for copy in copies[x]:
            copy.wait()
        rows = x_ref[x]
        for i in range(2):
            keep[i] = keep[i] + nt(rows, w_ref[i, x])
            send[i] = send[i] + nt(rows, half_ref[i, x])
    for i in range(2):
        keep_ref[i] = keep[i]
    fetch_out = pltpu.make_async_copy(keep_ref, keep_hbm, sem.at[0])
    fetch_out.start()
    for i in range(2):
        send_ref[i] = send[i].astype(BF)
    fetch_out.wait()


def grad_kernel(keep_hbm, got_hbm, in_hbm, a_hbm, out_ref, ga_ref, v_ref, keep_ref, got_ref, in_ref, a_ref, sems):
    fetch([(keep_hbm, keep_ref), (got_hbm, got_ref), (in_hbm, in_ref), (a_hbm, a_ref)], sems)
    units = keep_ref.shape[2]
    gate = keep_ref[0] + got_ref[0].astype(F32)
    up = keep_ref[1] + got_ref[1].astype(F32)
    sigma = jax.nn.sigmoid(gate)
    active = gate * sigma
    hidden = (active * up).astype(BF)
    v_ref[...] = nt(hidden, a_ref[...]).astype(BF)
    total = in_ref[0].astype(F32)
    for x in range(1, in_ref.shape[0]):
        total += in_ref[x].astype(F32)
    low_u = total[:, units:].astype(BF)
    grad = total[:, :units] + nn(low_u, a_ref[...])
    ga_ref[...] = tn(low_u, hidden)
    out_ref[0] = (grad * up * sigma * (1.0 + gate * (1.0 - sigma))).astype(BF)
    out_ref[1] = (grad * active).astype(BF)


def back_kernel(me_ref, g_ref, h_ref, wg_ref, wu_ref, swap_ref, out_ref):
    core = me_ref[1]
    chips, _, width = out_ref.shape
    for x in range(chips):
        cols = lanes(2 * x + core, width)
        term = nn(g_ref[0], wg_ref[:, cols]) + nn(g_ref[1], wu_ref[:, cols])
        term += nn(h_ref[0], swap_ref[0, x]) + nn(h_ref[1], swap_ref[1, x])
        out_ref[x] = term.astype(BF)


def total_kernel(in_ref, out_ref):
    experts = out_ref.shape[0]
    width = in_ref.shape[2]
    for s in range(CAP):
        rows = slice(s * experts, (s + 1) * experts)
        total = in_ref[0, rows].astype(F32)
        for x in range(1, in_ref.shape[0]):
            total += in_ref[x, rows].astype(F32)
        out_ref[:, s * width : (s + 1) * width] = total.astype(BF)


def pair_kernel(a_ref, b_ref, o_ref):
    o_ref[...] = (a_ref[...].astype(F32) + b_ref[...].astype(F32)).astype(BF)


def adapter_kernel(ids_ref, v0_ref, v1_ref, v2_ref, v3_ref, s_ref, o_ref, code_ref):
    code_ref[...] = code_of(ids_ref[...], code_ref.shape[0])
    low = v0_ref[...].astype(F32) + v1_ref[...].astype(F32)
    low += v2_ref[...].astype(F32) + v3_ref[...].astype(F32)
    o_ref[...] = tn(low.astype(BF), s_ref[...])


def combine_kernel(code_ref, r_ref, o_ref):
    width = o_ref.shape[1]
    total = jnp.zeros(o_ref.shape, F32)
    for s in range(CAP):
        pick = jnp.where(code_ref[...] == float(s), 1.0, 0.0).astype(BF)
        total += tn(pick, r_ref[:, s * width : (s + 1) * width])
    o_ref[...] = total.astype(BF)


def call(body, outs, *args, scalars=0, places=(), ends=(), scratch=()):
    vmem = pl.BlockSpec(memory_space=pltpu.VMEM)
    smem = pl.BlockSpec(memory_space=pltpu.SMEM)
    places = places or [vmem] * (len(args) - scalars)
    return pl.pallas_call(
        body,
        out_shape=outs,
        in_specs=[smem] * scalars + list(places),
        out_specs=ends or jax.tree.map(lambda _: vmem, outs),
        scratch_shapes=list(scratch),
        compiler_params=PARAMS,
    )(*args)


def per_device(tokens, grad_out, prob, ids, w_gate, w_up, w_down, adapter_a, adapter_b):
    experts = lax.axis_size(("z", "y"))
    chips = lax.axis_size("x")
    count, width = tokens.shape
    rank = adapter_b.shape[1]
    units = w_gate.shape[1]
    routes = experts * CAP
    w_gate, w_up, w_down, adapter_a, adapter_b = (
        w_gate[0], w_up[0], w_down[0], adapter_a[0], adapter_b[0],
    )
    sds = jax.ShapeDtypeStruct
    me = jnp.stack([lax.axis_index("x"), lax.axis_index("c")]).astype(jnp.int32)

    def swap(block):
        return lax.ppermute(block, "c", [(0, 1), (1, 0)])

    def shift(block, by):
        return lax.ppermute(block, "x", [(i, (i + by) % chips) for i in range(chips)])

    def over_x(block):
        return lax.all_to_all(block, "x", 0, 0, tiled=True)

    def route(block):
        return lax.all_to_all(block, ("z", "y"), 0, 0, tiled=True)

    parts = 2 * width // LANE
    slow = pl.BlockSpec(memory_space=pltpu.HBM)

    def pin(*arrays):
        return [pltpu.with_memory_space_constraint(x, pltpu.HBM) for x in arrays]

    near = pl.BlockSpec(memory_space=pltpu.VMEM)
    far = pl.BlockSpec(memory_space=pltpu.HBM)
    dma = pltpu.SemaphoreType.DMA

    packed = call(
        pack_kernel, sds((experts * parts, CAP * LANE), BF),
        *pin(ids.T, prob.T, tokens, grad_out),
        places=[slow] * 4,
        scratch=[
            pltpu.VMEM(ids.T.shape, ids.dtype), pltpu.VMEM(prob.T.shape, F32),
            pltpu.VMEM(tokens.shape, BF), pltpu.VMEM(tokens.shape, BF), dma((4,)),
        ],
    )
    arrived = route(packed.reshape(experts, parts, CAP * LANE))

    half, *down = call(
        prep_kernel,
        (sds((2, chips, units, width), BF),) + (sds((units, 2 * width), BF),) * 4,
        me, w_gate, w_up, w_down, scalars=1,
    )
    half = swap(half)
    down = down[:1] + [shift(block, d + 1) for d, block in enumerate(down[1:])]
    b_other = swap(adapter_b)
    arrived, half, b_other, *down = lax.optimization_barrier((arrived, half, b_other, *down))

    x_four, s_own = call(
        split_kernel, (pltpu.HBM((chips, routes, width), BF), pltpu.HBM((routes, width), BF)),
        arrived.reshape(experts * parts, CAP * LANE),
        ends=(far, far),
        scratch=[pltpu.VMEM((routes, width), BF)] * 2 + [dma((chips + 1,))],
    )
    x_all = over_x(x_four)
    s_other = swap(s_own)
    shares = (chips, routes, units + rank)
    sources = (s_own, s_other, adapter_b, b_other, *down)
    part = call(
        part_kernel, pltpu.HBM(shares, BF), me, *pin(*sources), scalars=1,
        places=[slow] * len(sources), ends=far,
        scratch=[pltpu.VMEM(x.shape, BF) for x in (*sources, sds(shares, BF))] + [dma((len(sources),))],
    )
    sums = over_x(part)
    keep, send = call(
        gate_kernel,
        (pltpu.HBM((2, routes, units), F32), sds((2, routes, units), BF)),
        me, *pin(x_all, w_gate, w_up, half), scalars=1, places=[slow] * 4, ends=(far, near),
        scratch=[
            pltpu.VMEM(x_all.shape, BF), pltpu.VMEM((2, chips, units, width), BF),
            pltpu.VMEM(half.shape, BF), pltpu.VMEM((2, routes, units), F32), dma((chips, 4)), dma((1,)),
        ],
    )
    got = swap(send)
    sources = (keep, got, sums, adapter_a)
    grads, grad_a, v_own = call(
        grad_kernel,
        (sds((2, routes, units), BF), sds((rank, units), F32), sds((routes, rank), BF)),
        *pin(*sources), places=[slow] * 4,
        scratch=[pltpu.VMEM(x.shape, x.dtype) for x in sources] + [dma((4,))],
    )
    grads_other = swap(grads)
    back = call(
        back_kernel, sds((chips, routes, width), BF),
        me, grads, grads_other, w_gate, w_up, half, scalars=1,
    )
    backs = over_x(back)
    total = call(total_kernel, sds((experts, CAP * width), BF), backs)
    home = route(total.reshape(experts, 2, CAP * width // 2)).reshape(experts, CAP * width)

    v_pair = call(pair_kernel, sds((routes, rank), BF), v_own, swap(v_own))
    v_all = [v_pair] + [shift(v_pair, d) for d in (1, 2, 3)]
    grad_b, code = call(
        adapter_kernel, (sds((rank, width), F32), sds((experts, count), F32)), ids.T, *v_all, s_own
    )
    out = call(combine_kernel, sds(tokens.shape, BF), code, home)
    return out, grad_a[None], grad_b[None]


def solution(mesh):
    fine = Mesh(mesh.devices.reshape(4, 2, 16, 4), ("x", "c", "z", "y"))
    dp, ex = ("x", "c"), ("z", "y")
    specs = (
        P(ex, dp), P(ex, dp), P(ex, None), P(ex, None),
        P(ex, dp, None), P(ex, dp, None), P(ex, dp, None), P(ex, None, dp), P(ex, None, dp),
    )
    return jax.shard_map(
        per_device,
        mesh=fine,
        in_specs=specs,
        out_specs=(P(ex, dp), P(ex, None, dp), P(ex, None, dp)),
        check_vma=False,
    )
```

```python
import jax
import jax.numpy as jnp
from jax import lax
from jax.experimental import pallas as pl
from jax.experimental.pallas import tpu as pltpu
from jax.sharding import Mesh, PartitionSpec as P

CAP = 5
BF = jnp.bfloat16
F32 = jnp.float32
LANE = 128
PARAMS = pltpu.CompilerParams(vmem_limit_bytes=16 * 1024 * 1024)


def nt(left, right):
    return lax.dot_general(left, right, (((1,), (1,)), ((), ())), preferred_element_type=F32)


def tn(left, right):
    return lax.dot_general(left, right, (((0,), (0,)), ((), ())), preferred_element_type=F32)


def nn(left, right):
    return jnp.dot(left, right, preferred_element_type=F32)


def lanes(index, width):
    return pl.ds(pl.multiple_of(index * width, width), width)


def fetch(pairs, sems):
    copies = [pltpu.make_async_copy(src, dst, sems.at[i]) for i, (src, dst) in enumerate(pairs)]
    for copy in copies:
        copy.start()
    for copy in copies:
        copy.wait()


def pack_kernel(ids_hbm, prob_hbm, tok_hbm, dy_hbm, out_ref, ids_ref, prob_ref, tok_ref, dy_ref, sems):
    fetch(
        [(ids_hbm, ids_ref), (prob_hbm, prob_ref), (tok_hbm, tok_ref), (dy_hbm, dy_ref)], sems
    )
    rows = out_ref.shape[0]
    count, width = tok_ref.shape
    parts = 2 * width // LANE
    span = parts * count
    row = lax.broadcasted_iota(jnp.int32, (rows, count), 0)
    own = lax.div(row, parts)
    hit = jnp.zeros((rows, count), F32)
    weight = jnp.zeros((rows, count), F32)
    for k in range(ids_ref.shape[0]):
        same = ids_ref[k : k + 1, :] == own
        hit = jnp.where(same, 1.0, hit)
        weight = jnp.where(same, prob_ref[k : k + 1, :], weight)
    weight = jnp.where(lax.rem(row, parts) < parts // 2, hit, weight)
    first = lax.broadcasted_iota(jnp.int32, (count, count), 0)
    second = lax.broadcasted_iota(jnp.int32, (count, count), 1)
    before = jnp.where(first < second, 1.0, 0.0).astype(BF)
    code = jnp.where(hit > 0.5, nn(hit.astype(BF), before), -1.0)
    wide_row = lax.broadcasted_iota(jnp.int32, (rows, span), 0)
    lane = lax.broadcasted_iota(jnp.int32, (rows, span), 1)
    here = lax.rem(wide_row, parts) == lax.div(lane, count)
    spread = jnp.where(here, jnp.concatenate([code] * parts, axis=1), -1.0)
    table = jnp.concatenate(
        [ref[:, c : c + LANE] for ref in (tok_ref, dy_ref) for c in range(0, width, LANE)], axis=0
    )
    for s in range(CAP):
        pick = jnp.where(spread == float(s), 1.0, 0.0).astype(BF)
        scale = jnp.sum(jnp.where(code == float(s), weight, 0.0), axis=1, keepdims=True)
        out_ref[:, s * LANE : (s + 1) * LANE] = (nn(pick, table) * scale).astype(BF)


def code_of(ids, experts):
    count = ids.shape[1]
    own = lax.broadcasted_iota(jnp.int32, (experts, count), 0)
    hit = jnp.zeros((experts, count), F32)
    for k in range(ids.shape[0]):
        hit = jnp.where(ids[k : k + 1, :] == own, 1.0, hit)
    first = lax.broadcasted_iota(jnp.int32, (count, count), 0)
    second = lax.broadcasted_iota(jnp.int32, (count, count), 1)
    before = jnp.where(first < second, 1.0, 0.0).astype(BF)
    return jnp.where(hit > 0.5, nn(hit.astype(BF), before), -1.0)


def split_kernel(in_ref, x_hbm, s_hbm, x_ref, s_ref, sems):
    total = in_ref.shape[0]
    width = s_ref.shape[1]
    parts = 2 * width // LANE
    experts = total // parts
    first = lax.broadcasted_iota(jnp.int32, (total, total), 0)
    second = lax.broadcasted_iota(jnp.int32, (total, total), 1)
    there = lax.rem(first, experts) * parts + lax.div(first, experts)
    perm = jnp.where(second == there, 1.0, 0.0).astype(BF)
    rows = nn(perm, in_ref[...]).astype(BF)
    for r in range(parts):
        ref = x_ref if r < parts // 2 else s_ref
        at = (r % (parts // 2)) * LANE
        for s in range(CAP):
            ref[s * experts : (s + 1) * experts, at : at + LANE] = rows[
                r * experts : (r + 1) * experts, s * LANE : (s + 1) * LANE
            ]
    chips = x_hbm.shape[0]
    fetch([(x_ref, x_hbm.at[x]) for x in range(chips)] + [(s_ref, s_hbm)], sems)


def prep_kernel(me_ref, wg_ref, wu_ref, wd_ref, swap_ref, d0_ref, d1_ref, d2_ref, d3_ref):
    chip, core = me_ref[0], me_ref[1]
    chips, units, width = swap_ref.shape[1:]
    for x in range(chips):
        cols = lanes(2 * x + 1 - core, width)
        swap_ref[0, x] = wg_ref[:, cols]
        swap_ref[1, x] = wu_ref[:, cols]
    for d, ref in enumerate((d0_ref, d1_ref, d2_ref, d3_ref)):
        ref[...] = wd_ref[:, lanes(lax.rem(chip + d, chips), 2 * width)]


def part_kernel(me_ref, *refs):
    chip, core = me_ref[0], me_ref[1]
    sources, out_hbm, held, out_ref, sems = refs[:8], refs[8], refs[9:17], refs[17], refs[18]
    fetch(list(zip(sources, held)), sems)
    s_ref, t_ref, b_ref, o_ref = held[:4]
    units, width = held[4].shape[0], s_ref.shape[1]
    chips = out_ref.shape[0]
    mine, other = s_ref[...], t_ref[...]
    low = (nt(mine, b_ref[...]) + nt(other, o_ref[...])).astype(BF)
    for d, ref in enumerate(held[4:]):
        w_mine, w_other = ref[:, lanes(core, width)], ref[:, lanes(1 - core, width)]
        to = lax.rem(chip + chips - d, chips)
        out_ref[to, :, :units] = (nt(mine, w_mine) + nt(other, w_other)).astype(BF)
        out_ref[to, :, units:] = low
    fetch([(out_ref, out_hbm)], sems)


def stream(half_hbm, half_ref, sems):
    copies = [
        pltpu.make_async_copy(half_hbm.at[:, x], half_ref.at[:, x], sems.at[x])
        for x in range(half_ref.shape[1])
    ]
    for copy in copies:
        copy.start()
    return copies


def gate_kernel(
    me_ref, x_ref, wg_ref, wu_ref, half_hbm, keep_hbm, send_ref, half_ref, keep_ref, sems, sem
):
    core = me_ref[1]
    chips, routes, width = x_ref.shape
    units = wg_ref.shape[0]
    copies = stream(half_hbm, half_ref, sems)
    keep = [jnp.zeros((routes, units), F32)] * 2
    send = [jnp.zeros((routes, units), F32)] * 2
    for x in range(chips):
        cols = lanes(2 * x + core, width)
        keep[0] = keep[0] + nt(x_ref[x], wg_ref[:, cols])
        keep[1] = keep[1] + nt(x_ref[x], wu_ref[:, cols])
    for i in range(2):
        keep_ref[i] = keep[i]
    store = pltpu.make_async_copy(keep_ref, keep_hbm, sem.at[0])
    store.start()
    for x in range(chips):
        copies[x].wait()
        for i in range(2):
            send[i] = send[i] + nt(x_ref[x], half_ref[i, x])
    for i in range(2):
        send_ref[i] = send[i].astype(BF)
    store.wait()


def grad_kernel(keep_hbm, got_ref, in_ref, a_ref, out_ref, ga_ref, keep_ref, sem):
    fetch_keep = pltpu.make_async_copy(keep_hbm, keep_ref, sem.at[0])
    fetch_keep.start()
    units = keep_ref.shape[2]
    total = in_ref[0].astype(F32)
    for x in range(1, in_ref.shape[0]):
        total += in_ref[x].astype(F32)
    low_u = total[:, units:].astype(BF)
    grad = total[:, :units] + nn(low_u, a_ref[...])
    fetch_keep.wait()
    gate = keep_ref[0] + got_ref[0].astype(F32)
    up = keep_ref[1] + got_ref[1].astype(F32)
    sigma = jax.nn.sigmoid(gate)
    active = gate * sigma
    hidden = (active * up).astype(BF)
    ga_ref[...] = tn(low_u, hidden)
    grad_gate = (grad * up * sigma * (1.0 + gate * (1.0 - sigma))).astype(BF)
    grad_up = (grad * active).astype(BF)
    low_v = nt(hidden, a_ref[...]).astype(BF)
    out_ref[...] = jnp.concatenate([grad_gate, grad_up, low_v], axis=1)


def back_kernel(
    me_ref, g_ref, h_ref, wg_ref, wu_ref, half_hbm, out_hbm, v_ref, half_ref, out_ref, sems, out_sems
):
    core = me_ref[1]
    chips, _, width = out_ref.shape
    units = wg_ref.shape[0]
    copies = stream(half_hbm, half_ref, sems)
    mine = [g_ref[:, i * units : (i + 1) * units] for i in range(2)]
    other = [h_ref[:, i * units : (i + 1) * units] for i in range(2)]
    stores = []
    v_ref[...] = (g_ref[:, 2 * units :].astype(F32) + h_ref[:, 2 * units :].astype(F32)).astype(BF)
    for x in range(chips):
        cols = lanes(2 * x + core, width)
        term = nn(mine[0], wg_ref[:, cols]) + nn(mine[1], wu_ref[:, cols])
        copies[x].wait()
        term += nn(other[0], half_ref[0, x]) + nn(other[1], half_ref[1, x])
        out_ref[x] = term.astype(BF)
        stores.append(pltpu.make_async_copy(out_ref.at[x], out_hbm.at[x], out_sems.at[x]))
        stores[x].start()
    for store in stores:
        store.wait()


def code_kernel(ids_ref, code_ref):
    code_ref[...] = code_of(ids_ref[...], code_ref.shape[0])


def total_kernel(in_ref, out_ref):
    experts = out_ref.shape[0]
    width = in_ref.shape[2]
    for s in range(CAP):
        rows = slice(s * experts, (s + 1) * experts)
        total = in_ref[0, rows].astype(F32)
        for x in range(1, in_ref.shape[0]):
            total += in_ref[x, rows].astype(F32)
        out_ref[:, s * width : (s + 1) * width] = total.astype(BF)


def adapter_kernel(v0_ref, v1_ref, v2_ref, v3_ref, s_ref, o_ref):
    low = v0_ref[...].astype(F32) + v1_ref[...].astype(F32)
    low += v2_ref[...].astype(F32) + v3_ref[...].astype(F32)
    o_ref[...] = tn(low.astype(BF), s_ref[...])


def combine_kernel(code_ref, r_ref, o_ref):
    width = o_ref.shape[1]
    total = jnp.zeros(o_ref.shape, F32)
    for s in range(CAP):
        pick = jnp.where(code_ref[...] == float(s), 1.0, 0.0).astype(BF)
        total += tn(pick, r_ref[:, s * width : (s + 1) * width])
    o_ref[...] = total.astype(BF)


def call(body, outs, *args, scalars=0, places=(), ends=(), scratch=()):
    vmem = pl.BlockSpec(memory_space=pltpu.VMEM)
    smem = pl.BlockSpec(memory_space=pltpu.SMEM)
    places = places or [vmem] * (len(args) - scalars)
    return pl.pallas_call(
        body,
        out_shape=outs,
        in_specs=[smem] * scalars + list(places),
        out_specs=ends or jax.tree.map(lambda _: vmem, outs),
        scratch_shapes=list(scratch),
        compiler_params=PARAMS,
    )(*args)


def per_device(tokens, grad_out, prob, ids, w_gate, w_up, w_down, adapter_a, adapter_b):
    experts = lax.axis_size(("z", "y"))
    chips = lax.axis_size("x")
    count, width = tokens.shape
    rank = adapter_b.shape[1]
    units = w_gate.shape[1]
    routes = experts * CAP
    w_gate, w_up, w_down, adapter_a, adapter_b = (
        w_gate[0], w_up[0], w_down[0], adapter_a[0], adapter_b[0],
    )
    sds = jax.ShapeDtypeStruct
    me = jnp.stack([lax.axis_index("x"), lax.axis_index("c")]).astype(jnp.int32)

    def swap(block):
        return lax.ppermute(block, "c", [(0, 1), (1, 0)])

    def shift(block, by):
        return lax.ppermute(block, "x", [(i, (i + by) % chips) for i in range(chips)])

    def over_x(block):
        return lax.all_to_all(block, "x", 0, 0, tiled=True)

    def route(block):
        return lax.all_to_all(block, ("z", "y"), 0, 0, tiled=True)

    parts = 2 * width // LANE
    slow = pl.BlockSpec(memory_space=pltpu.HBM)

    def pin(*arrays):
        return [pltpu.with_memory_space_constraint(x, pltpu.HBM) for x in arrays]

    near = pl.BlockSpec(memory_space=pltpu.VMEM)
    far = pl.BlockSpec(memory_space=pltpu.HBM)
    dma = pltpu.SemaphoreType.DMA

    packed = call(
        pack_kernel, sds((experts * parts, CAP * LANE), BF),
        *pin(ids.T, prob.T, tokens, grad_out),
        places=[slow] * 4,
        scratch=[
            pltpu.VMEM(ids.T.shape, ids.dtype), pltpu.VMEM(prob.T.shape, F32),
            pltpu.VMEM(tokens.shape, BF), pltpu.VMEM(tokens.shape, BF), dma((4,)),
        ],
    )
    arrived = route(packed.reshape(experts, parts, CAP * LANE))

    half, *down = call(
        prep_kernel,
        (sds((2, chips, units, width), BF),) + (sds((units, 2 * width), BF),) * 4,
        me, w_gate, w_up, w_down, scalars=1,
    )
    half = swap(half)
    down = down[:1] + [shift(block, d + 1) for d, block in enumerate(down[1:])]
    b_other = swap(adapter_b)
    arrived, half, b_other, *down = lax.optimization_barrier((arrived, half, b_other, *down))

    x_four, s_own = call(
        split_kernel, (pltpu.HBM((chips, routes, width), BF), pltpu.HBM((routes, width), BF)),
        arrived.reshape(experts * parts, CAP * LANE),
        ends=(far, far),
        scratch=[pltpu.VMEM((routes, width), BF)] * 2 + [dma((chips + 1,))],
    )
    x_all = over_x(x_four)
    s_other = swap(s_own)
    shares = (chips, routes, units + rank)
    sources = (s_own, s_other, adapter_b, b_other, *down)
    part = call(
        part_kernel, pltpu.HBM(shares, BF), me, *pin(*sources), scalars=1,
        places=[slow] * len(sources), ends=far,
        scratch=[pltpu.VMEM(x.shape, BF) for x in (*sources, sds(shares, BF))] + [dma((len(sources),))],
    )
    sums = over_x(part)
    keep, send = call(
        gate_kernel,
        (pltpu.HBM((2, routes, units), F32), sds((2, routes, units), BF)),
        me, x_all, w_gate, w_up, *pin(half), scalars=1, places=[near] * 3 + [slow], ends=(far, near),
        scratch=[
            pltpu.VMEM(half.shape, BF), pltpu.VMEM((2, routes, units), F32), dma((chips,)), dma((1,)),
        ],
    )
    got = swap(send)
    grads, grad_a = call(
        grad_kernel,
        (sds((routes, 2 * units + rank), BF), sds((rank, units), F32)),
        *pin(keep), got, sums, adapter_a, places=[slow] + [near] * 3,
        scratch=[pltpu.VMEM(keep.shape, F32), dma((1,))],
    )
    grads_other = swap(grads)
    back_shape = (chips, routes, width)
    back, v_pair = call(
        back_kernel, (pltpu.HBM((chips, routes, width), BF), sds((routes, rank), BF)),
        me, grads, grads_other, w_gate, w_up, *pin(half), scalars=1, places=[near] * 4 + [slow],
        ends=(far, near),
        scratch=[pltpu.VMEM(half.shape, BF), pltpu.VMEM(back_shape, BF), dma((chips,)), dma((chips,))],
    )
    code = call(code_kernel, sds((experts, count), F32), ids.T)
    backs, code = lax.optimization_barrier((over_x(back), code))
    total = call(total_kernel, sds((experts, CAP * width), BF), backs)
    home = route(total.reshape(experts, 2, CAP * width // 2)).reshape(experts, CAP * width)

    v_all = [v_pair] + [shift(v_pair, d) for d in (1, 2, 3)]
    grad_b = call(adapter_kernel, sds((rank, width), F32), *v_all, s_own)
    out = call(combine_kernel, sds(tokens.shape, BF), code, home)
    return out, grad_a[None], grad_b[None]


def solution(mesh):
    fine = Mesh(mesh.devices.reshape(4, 2, 16, 4), ("x", "c", "z", "y"))
    dp, ex = ("x", "c"), ("z", "y")
    specs = (
        P(ex, dp), P(ex, dp), P(ex, None), P(ex, None),
        P(ex, dp, None), P(ex, dp, None), P(ex, dp, None), P(ex, None, dp), P(ex, None, dp),
    )
    return jax.shard_map(
        per_device,
        mesh=fine,
        in_specs=specs,
        out_specs=(P(ex, dp), P(ex, None, dp), P(ex, None, dp)),
        check_vma=False,
    )
```

```python
import jax
import jax.numpy as jnp
from jax import lax
from jax.experimental import pallas as pl
from jax.experimental.pallas import tpu as pltpu
from jax.sharding import Mesh, PartitionSpec as P

CAP = 5
BF = jnp.bfloat16
F32 = jnp.float32
LANE = 128
FLAT = 4
PARAMS = pltpu.CompilerParams(vmem_limit_bytes=16 * 1024 * 1024)


def nt(left, right):
    return lax.dot_general(left, right, (((1,), (1,)), ((), ())), preferred_element_type=F32)


def tn(left, right):
    return lax.dot_general(left, right, (((0,), (0,)), ((), ())), preferred_element_type=F32)


def nn(left, right):
    return jnp.dot(left, right, preferred_element_type=F32)


def lanes(index, width):
    return pl.ds(pl.multiple_of(index * width, width), width)


def fetch(pairs, sems):
    copies = [pltpu.make_async_copy(src, dst, sems.at[i]) for i, (src, dst) in enumerate(pairs)]
    for copy in copies:
        copy.start()
    for copy in copies:
        copy.wait()


def expert_of(place, experts):
    deep = experts // FLAT
    return lax.rem(place, deep) * FLAT + lax.div(place, deep)


def pack_kernel(ids_hbm, prob_hbm, tok_hbm, dy_hbm, out_ref, ids_ref, prob_ref, tok_ref, dy_ref, sems):
    fetch(
        [(ids_hbm, ids_ref), (prob_hbm, prob_ref), (tok_hbm, tok_ref), (dy_hbm, dy_ref)], sems
    )
    rows = out_ref.shape[0]
    count, width = tok_ref.shape
    parts = 2 * width // LANE
    span = parts * count
    row = lax.broadcasted_iota(jnp.int32, (rows, count), 0)
    own = expert_of(lax.div(row, parts), rows // parts)
    hit = jnp.zeros((rows, count), F32)
    weight = jnp.zeros((rows, count), F32)
    for k in range(ids_ref.shape[0]):
        same = ids_ref[k : k + 1, :] == own
        hit = jnp.where(same, 1.0, hit)
        weight = jnp.where(same, prob_ref[k : k + 1, :], weight)
    weight = jnp.where(lax.rem(row, parts) < parts // 2, hit, weight)
    first = lax.broadcasted_iota(jnp.int32, (count, count), 0)
    second = lax.broadcasted_iota(jnp.int32, (count, count), 1)
    before = jnp.where(first < second, 1.0, 0.0).astype(BF)
    code = jnp.where(hit > 0.5, nn(hit.astype(BF), before), -1.0)
    wide_row = lax.broadcasted_iota(jnp.int32, (rows, span), 0)
    lane = lax.broadcasted_iota(jnp.int32, (rows, span), 1)
    here = lax.rem(wide_row, parts) == lax.div(lane, count)
    spread = jnp.where(here, jnp.concatenate([code] * parts, axis=1), -1.0)
    table = jnp.concatenate(
        [ref[:, c : c + LANE] for ref in (tok_ref, dy_ref) for c in range(0, width, LANE)], axis=0
    )
    for s in range(CAP):
        pick = jnp.where(spread == float(s), 1.0, 0.0).astype(BF)
        scale = jnp.sum(jnp.where(code == float(s), weight, 0.0), axis=1, keepdims=True)
        out_ref[:, s * LANE : (s + 1) * LANE] = (nn(pick, table) * scale).astype(BF)


def code_of(ids, experts):
    count = ids.shape[1]
    own = expert_of(lax.broadcasted_iota(jnp.int32, (experts, count), 0), experts)
    hit = jnp.zeros((experts, count), F32)
    for k in range(ids.shape[0]):
        hit = jnp.where(ids[k : k + 1, :] == own, 1.0, hit)
    first = lax.broadcasted_iota(jnp.int32, (count, count), 0)
    second = lax.broadcasted_iota(jnp.int32, (count, count), 1)
    before = jnp.where(first < second, 1.0, 0.0).astype(BF)
    return jnp.where(hit > 0.5, nn(hit.astype(BF), before), -1.0)


def split_kernel(in_ref, x_hbm, s_hbm, x_ref, s_ref, sems):
    total = in_ref.shape[0]
    width = s_ref.shape[1]
    parts = 2 * width // LANE
    experts = total // parts
    first = lax.broadcasted_iota(jnp.int32, (total, total), 0)
    second = lax.broadcasted_iota(jnp.int32, (total, total), 1)
    there = lax.rem(first, experts) * parts + lax.div(first, experts)
    perm = jnp.where(second == there, 1.0, 0.0).astype(BF)
    rows = nn(perm, in_ref[...]).astype(BF)
    for r in range(parts):
        ref = x_ref if r < parts // 2 else s_ref
        at = (r % (parts // 2)) * LANE
        for s in range(CAP):
            ref[s * experts : (s + 1) * experts, at : at + LANE] = rows[
                r * experts : (r + 1) * experts, s * LANE : (s + 1) * LANE
            ]
    chips = x_hbm.shape[0]
    fetch([(x_ref, x_hbm.at[x]) for x in range(chips)] + [(s_ref, s_hbm)], sems)


def prep_kernel(me_ref, wg_ref, wu_ref, wd_ref, own_ref, swap_ref, d0_ref, d1_ref, d2_ref, d3_ref):
    chip, core = me_ref[0], me_ref[1]
    chips, units, width = swap_ref.shape[1:]
    for d, ref in enumerate((d0_ref, d1_ref, d2_ref, d3_ref)):
        ref[...] = wd_ref[:, lanes(lax.rem(chip + d, chips), 2 * width)]
    for x in range(chips):
        for ref, which in ((own_ref, core), (swap_ref, 1 - core)):
            cols = lanes(2 * x + which, width)
            ref[0, x] = wg_ref[:, cols]
            ref[1, x] = wu_ref[:, cols]


def part_kernel(me_ref, *refs):
    chip, core = me_ref[0], me_ref[1]
    sources, out_hbm, held, out_ref, sems = refs[:8], refs[8], refs[9:17], refs[17], refs[18]
    fetch(list(zip(sources, held)), sems)
    s_ref, t_ref, b_ref, o_ref = held[:4]
    units, width = held[4].shape[0], s_ref.shape[1]
    chips = out_ref.shape[0]
    mine, other = s_ref[...], t_ref[...]
    low = (nt(mine, b_ref[...]) + nt(other, o_ref[...])).astype(BF)
    for d, ref in enumerate(held[4:]):
        w_mine, w_other = ref[:, lanes(core, width)], ref[:, lanes(1 - core, width)]
        to = lax.rem(chip + chips - d, chips)
        out_ref[to, :, :units] = (nt(mine, w_mine) + nt(other, w_other)).astype(BF)
        out_ref[to, :, units:] = low
    fetch([(out_ref, out_hbm)], sems)


def gate_kernel(x_ref, own_ref, half_ref, keep_hbm, send_ref, keep_ref, sem):
    chips, routes, width = x_ref.shape
    units = own_ref.shape[2]
    keep = [jnp.zeros((routes, units), F32)] * 2
    send = [jnp.zeros((routes, units), F32)] * 2
    for x in range(chips):
        for i in range(2):
            keep[i] = keep[i] + nt(x_ref[x], own_ref[i, x])
    for i in range(2):
        keep_ref[i] = keep[i]
    store = pltpu.make_async_copy(keep_ref, keep_hbm, sem.at[0])
    store.start()
    for x in range(chips):
        for i in range(2):
            send[i] = send[i] + nt(x_ref[x], half_ref[i, x])
    for i in range(2):
        send_ref[i] = send[i].astype(BF)
    store.wait()


def grad_kernel(keep_hbm, got_hbm, in_hbm, a_hbm, out_ref, ga_ref, keep_ref, got_ref, in_ref, a_ref, sems):
    fetch([(keep_hbm, keep_ref), (got_hbm, got_ref), (in_hbm, in_ref), (a_hbm, a_ref)], sems)
    units = keep_ref.shape[2]
    total = in_ref[0].astype(F32)
    for x in range(1, in_ref.shape[0]):
        total += in_ref[x].astype(F32)
    low_u = total[:, units:].astype(BF)
    grad = total[:, :units] + nn(low_u, a_ref[...])
    gate = keep_ref[0] + got_ref[0].astype(F32)
    up = keep_ref[1] + got_ref[1].astype(F32)
    sigma = jax.nn.sigmoid(gate)
    active = gate * sigma
    hidden = (active * up).astype(BF)
    ga_ref[...] = tn(low_u, hidden)
    out_ref[:, :units] = (grad * up * sigma * (1.0 + gate * (1.0 - sigma))).astype(BF)
    low_v = nt(hidden, a_ref[...]).astype(BF)
    out_ref[:, units:] = jnp.concatenate([(grad * active).astype(BF), low_v], axis=1)


def back_kernel(g_ref, h_ref, own_ref, half_ref, out_hbm, v_ref, out_ref, out_sems):
    chips = out_ref.shape[0]
    units = own_ref.shape[2]
    mine = [g_ref[:, i * units : (i + 1) * units] for i in range(2)]
    other = [h_ref[:, i * units : (i + 1) * units] for i in range(2)]
    stores = []
    for x in range(chips):
        term = nn(mine[0], own_ref[0, x]) + nn(mine[1], own_ref[1, x])
        term += nn(other[0], half_ref[0, x]) + nn(other[1], half_ref[1, x])
        out_ref[x] = term.astype(BF)
        stores.append(pltpu.make_async_copy(out_ref.at[x], out_hbm.at[x], out_sems.at[x]))
        stores[x].start()
    v_ref[...] = (g_ref[:, 2 * units :].astype(F32) + h_ref[:, 2 * units :].astype(F32)).astype(BF)
    for store in stores:
        store.wait()


def code_kernel(ids_ref, code_ref):
    code_ref[...] = code_of(ids_ref[...], code_ref.shape[0])


def total_kernel(in_ref, out_ref):
    experts = out_ref.shape[0]
    width = in_ref.shape[2]
    for s in range(CAP):
        rows = slice(s * experts, (s + 1) * experts)
        total = in_ref[0, rows].astype(F32)
        for x in range(1, in_ref.shape[0]):
            total += in_ref[x, rows].astype(F32)
        out_ref[:, s * width : (s + 1) * width] = total.astype(BF)


def adapter_kernel(v0_ref, v1_ref, v2_ref, v3_ref, s_ref, o_ref):
    low = v0_ref[...].astype(F32) + v1_ref[...].astype(F32)
    low += v2_ref[...].astype(F32) + v3_ref[...].astype(F32)
    o_ref[...] = tn(low.astype(BF), s_ref[...])


def combine_kernel(code_ref, r_ref, o_ref):
    width = o_ref.shape[1]
    total = jnp.zeros(o_ref.shape, F32)
    for s in range(CAP):
        pick = jnp.where(code_ref[...] == float(s), 1.0, 0.0).astype(BF)
        total += tn(pick, r_ref[:, s * width : (s + 1) * width])
    o_ref[...] = total.astype(BF)


def call(body, outs, *args, scalars=0, places=(), ends=(), scratch=()):
    vmem = pl.BlockSpec(memory_space=pltpu.VMEM)
    smem = pl.BlockSpec(memory_space=pltpu.SMEM)
    places = places or [vmem] * (len(args) - scalars)
    return pl.pallas_call(
        body,
        out_shape=outs,
        in_specs=[smem] * scalars + list(places),
        out_specs=ends or jax.tree.map(lambda _: vmem, outs),
        scratch_shapes=list(scratch),
        compiler_params=PARAMS,
    )(*args)


def per_device(tokens, grad_out, prob, ids, w_gate, w_up, w_down, adapter_a, adapter_b):
    experts = lax.axis_size(("z", "y"))
    chips = lax.axis_size("x")
    count, width = tokens.shape
    rank = adapter_b.shape[1]
    units = w_gate.shape[1]
    routes = experts * CAP
    w_gate, w_up, w_down, adapter_a, adapter_b = (
        w_gate[0], w_up[0], w_down[0], adapter_a[0], adapter_b[0],
    )
    sds = jax.ShapeDtypeStruct
    me = jnp.stack([lax.axis_index("x"), lax.axis_index("c")]).astype(jnp.int32)

    def swap(block):
        return lax.ppermute(block, "c", [(0, 1), (1, 0)])

    def shift(block, by):
        return lax.ppermute(block, "x", [(i, (i + by) % chips) for i in range(chips)])

    def over_x(block):
        return lax.all_to_all(block, "x", 0, 0, tiled=True)

    def route(block):
        return lax.all_to_all(block, ("y", "z"), 0, 0, tiled=True)

    parts = 2 * width // LANE
    slow = pl.BlockSpec(memory_space=pltpu.HBM)

    def pin(*arrays):
        return [pltpu.with_memory_space_constraint(x, pltpu.HBM) for x in arrays]

    near = pl.BlockSpec(memory_space=pltpu.VMEM)
    far = pl.BlockSpec(memory_space=pltpu.HBM)
    dma = pltpu.SemaphoreType.DMA

    packed = call(
        pack_kernel, sds((experts * parts, CAP * LANE), BF),
        *pin(ids.T, prob.T, tokens, grad_out),
        places=[slow] * 4,
        scratch=[
            pltpu.VMEM(ids.T.shape, ids.dtype), pltpu.VMEM(prob.T.shape, F32),
            pltpu.VMEM(tokens.shape, BF), pltpu.VMEM(tokens.shape, BF), dma((4,)),
        ],
    )
    arrived = route(packed.reshape(experts, parts, CAP * LANE))

    own_cols, half, *down = call(
        prep_kernel,
        (sds((2, chips, units, width), BF),) * 2 + (sds((units, 2 * width), BF),) * 4,
        me, w_gate, w_up, w_down, scalars=1,
    )
    half = swap(half)
    down = down[:1] + [shift(block, d + 1) for d, block in enumerate(down[1:])]
    b_other = swap(adapter_b)
    arrived, half, b_other, *down = lax.optimization_barrier((arrived, half, b_other, *down))

    x_four, s_own = call(
        split_kernel, (pltpu.HBM((chips, routes, width), BF), pltpu.HBM((routes, width), BF)),
        arrived.reshape(experts * parts, CAP * LANE),
        ends=(far, far),
        scratch=[pltpu.VMEM((routes, width), BF)] * 2 + [dma((chips + 1,))],
    )
    x_all = over_x(x_four)
    s_other = swap(s_own)
    shares = (chips, routes, units + rank)
    sources = (s_own, s_other, adapter_b, b_other, *down)
    part = call(
        part_kernel, pltpu.HBM(shares, BF), me, *pin(*sources), scalars=1,
        places=[slow] * len(sources), ends=far,
        scratch=[pltpu.VMEM(x.shape, BF) for x in (*sources, sds(shares, BF))] + [dma((len(sources),))],
    )
    sums = over_x(part)
    keep, send = call(
        gate_kernel,
        (pltpu.HBM((2, routes, units), F32), sds((2, routes, units), BF)),
        x_all, own_cols, half, ends=(far, near),
        scratch=[pltpu.VMEM((2, routes, units), F32), dma((1,))],
    )
    got = swap(send)
    sources = (keep, got, sums, adapter_a)
    grads, grad_a = call(
        grad_kernel,
        (sds((routes, 2 * units + rank), BF), sds((rank, units), F32)),
        *pin(*sources), places=[slow] * 4,
        scratch=[pltpu.VMEM(x.shape, x.dtype) for x in sources] + [dma((4,))],
    )
    grads_other = swap(grads)
    back_shape = (chips, routes, width)
    back, v_pair = call(
        back_kernel, (pltpu.HBM(back_shape, BF), sds((routes, rank), BF)),
        grads, grads_other, own_cols, half, ends=(far, near),
        scratch=[pltpu.VMEM(back_shape, BF), dma((chips,))],
    )
    code = call(code_kernel, sds((experts, count), F32), ids.T)
    backs, code = lax.optimization_barrier((over_x(back), code))
    total = call(total_kernel, sds((experts, CAP * width), BF), backs)
    home = route(total.reshape(experts, 2, CAP * width // 2)).reshape(experts, CAP * width)

    v_all = [v_pair] + [shift(v_pair, d) for d in (1, 2, 3)]
    grad_b = call(adapter_kernel, sds((rank, width), F32), *v_all, s_own)
    out = call(combine_kernel, sds(tokens.shape, BF), code, home)
    return out, grad_a[None], grad_b[None]


def solution(mesh):
    fine = Mesh(mesh.devices.reshape(4, 2, 16, 4), ("x", "c", "z", "y"))
    dp, ex = ("x", "c"), ("z", "y")
    specs = (
        P(ex, dp), P(ex, dp), P(ex, None), P(ex, None),
        P(ex, dp, None), P(ex, dp, None), P(ex, dp, None), P(ex, None, dp), P(ex, None, dp),
    )
    return jax.shard_map(
        per_device,
        mesh=fine,
        in_specs=specs,
        out_specs=(P(ex, dp), P(ex, None, dp), P(ex, None, dp)),
        check_vma=False,
    )
```

```python
import jax
import jax.numpy as jnp
from jax import lax
from jax.experimental import pallas as pl
from jax.experimental.pallas import tpu as pltpu
from jax.sharding import Mesh, PartitionSpec as P

CAP = 5
BF = jnp.bfloat16
F32 = jnp.float32
LANE = 128
FLAT = 4
PARAMS = pltpu.CompilerParams(vmem_limit_bytes=16 * 1024 * 1024)


def nt(left, right):
    return lax.dot_general(left, right, (((1,), (1,)), ((), ())), preferred_element_type=F32)


def tn(left, right):
    return lax.dot_general(left, right, (((0,), (0,)), ((), ())), preferred_element_type=F32)


def nn(left, right):
    return jnp.dot(left, right, preferred_element_type=F32)


def lanes(index, width):
    return pl.ds(pl.multiple_of(index * width, width), width)


def fetch(pairs, sems):
    copies = [pltpu.make_async_copy(src, dst, sems.at[i]) for i, (src, dst) in enumerate(pairs)]
    for copy in copies:
        copy.start()
    for copy in copies:
        copy.wait()


def expert_of(place, experts):
    deep = experts // FLAT
    return lax.rem(place, deep) * FLAT + lax.div(place, deep)


def pack_kernel(ids_hbm, prob_hbm, tok_hbm, dy_hbm, out_ref, ids_ref, prob_ref, tok_ref, dy_ref, sems):
    fetch(
        [(ids_hbm, ids_ref), (prob_hbm, prob_ref), (tok_hbm, tok_ref), (dy_hbm, dy_ref)], sems
    )
    rows = out_ref.shape[0]
    count, width = tok_ref.shape
    parts = 2 * width // LANE
    span = parts * count
    row = lax.broadcasted_iota(jnp.int32, (rows, count), 0)
    own = expert_of(lax.div(row, parts), rows // parts)
    hit = jnp.zeros((rows, count), F32)
    weight = jnp.zeros((rows, count), F32)
    for k in range(ids_ref.shape[0]):
        same = ids_ref[k : k + 1, :] == own
        hit = jnp.where(same, 1.0, hit)
        weight = jnp.where(same, prob_ref[k : k + 1, :], weight)
    weight = jnp.where(lax.rem(row, parts) < parts // 2, hit, weight)
    first = lax.broadcasted_iota(jnp.int32, (count, count), 0)
    second = lax.broadcasted_iota(jnp.int32, (count, count), 1)
    before = jnp.where(first < second, 1.0, 0.0).astype(BF)
    code = jnp.where(hit > 0.5, nn(hit.astype(BF), before), -1.0)
    wide_row = lax.broadcasted_iota(jnp.int32, (rows, span), 0)
    lane = lax.broadcasted_iota(jnp.int32, (rows, span), 1)
    here = lax.rem(wide_row, parts) == lax.div(lane, count)
    spread = jnp.where(here, jnp.concatenate([code] * parts, axis=1), -1.0)
    table = jnp.concatenate(
        [ref[:, c : c + LANE] for ref in (tok_ref, dy_ref) for c in range(0, width, LANE)], axis=0
    )
    for s in range(CAP):
        pick = jnp.where(spread == float(s), 1.0, 0.0).astype(BF)
        scale = jnp.sum(jnp.where(code == float(s), weight, 0.0), axis=1, keepdims=True)
        out_ref[:, s * LANE : (s + 1) * LANE] = (nn(pick, table) * scale).astype(BF)


def split_kernel(in_ref, x_hbm, s_hbm, x_ref, s_ref, sems):
    total = in_ref.shape[0]
    width = s_ref.shape[1]
    parts = 2 * width // LANE
    experts = total // parts
    first = lax.broadcasted_iota(jnp.int32, (total, total), 0)
    second = lax.broadcasted_iota(jnp.int32, (total, total), 1)
    there = lax.rem(first, experts) * parts + lax.div(first, experts)
    perm = jnp.where(second == there, 1.0, 0.0).astype(BF)
    rows = nn(perm, in_ref[...]).astype(BF)
    for r in range(parts):
        ref = x_ref if r < parts // 2 else s_ref
        at = (r % (parts // 2)) * LANE
        for s in range(CAP):
            ref[s * experts : (s + 1) * experts, at : at + LANE] = rows[
                r * experts : (r + 1) * experts, s * LANE : (s + 1) * LANE
            ]
    chips = x_hbm.shape[0]
    fetch([(x_ref, x_hbm.at[x]) for x in range(chips)] + [(s_ref, s_hbm)], sems)


def prep_kernel(me_ref, wg_ref, wu_ref, wd_ref, own_ref, swap_ref, d0_ref, d1_ref, d2_ref, d3_ref):
    chip, core = me_ref[0], me_ref[1]
    chips, units, width = swap_ref.shape[1:]
    for d, ref in enumerate((d0_ref, d1_ref, d2_ref, d3_ref)):
        ref[...] = wd_ref[:, lanes(lax.rem(chip + d, chips), 2 * width)]
    for x in range(chips):
        for ref, which in ((own_ref, core), (swap_ref, 1 - core)):
            cols = lanes(2 * x + which, width)
            ref[0, x] = wg_ref[:, cols]
            ref[1, x] = wu_ref[:, cols]


def part_kernel(me_ref, *refs):
    chip, core = me_ref[0], me_ref[1]
    sources, out_hbm, held, out_ref, sems = refs[:8], refs[8], refs[9:17], refs[17], refs[18]
    fetch(list(zip(sources, held)), sems)
    s_ref, t_ref, b_ref, o_ref = held[:4]
    units, width = held[4].shape[0], s_ref.shape[1]
    chips = out_ref.shape[0]
    mine, other = s_ref[...], t_ref[...]
    low = (nt(mine, b_ref[...]) + nt(other, o_ref[...])).astype(BF)
    for d, ref in enumerate(held[4:]):
        w_mine, w_other = ref[:, lanes(core, width)], ref[:, lanes(1 - core, width)]
        to = lax.rem(chip + chips - d, chips)
        out_ref[to, :, :units] = (nt(mine, w_mine) + nt(other, w_other)).astype(BF)
        out_ref[to, :, units:] = low
    fetch([(out_ref, out_hbm)], sems)


def gate_kernel(x_ref, own_ref, half_ref, keep_hbm, send_ref, keep_ref, sem):
    chips, routes, width = x_ref.shape
    units = own_ref.shape[2]
    keep = [jnp.zeros((routes, units), F32)] * 2
    send = [jnp.zeros((routes, units), F32)] * 2
    for x in range(chips):
        for i in range(2):
            keep[i] = keep[i] + nt(x_ref[x], own_ref[i, x])
    for i in range(2):
        keep_ref[i] = keep[i]
    store = pltpu.make_async_copy(keep_ref, keep_hbm, sem.at[0])
    store.start()
    for x in range(chips):
        for i in range(2):
            send[i] = send[i] + nt(x_ref[x], half_ref[i, x])
    for i in range(2):
        send_ref[i] = send[i].astype(BF)
    store.wait()


def grad_kernel(keep_hbm, got_hbm, in_hbm, a_hbm, out_ref, ga_ref, keep_ref, got_ref, in_ref, a_ref, sems):
    fetch([(keep_hbm, keep_ref), (got_hbm, got_ref), (in_hbm, in_ref), (a_hbm, a_ref)], sems)
    units = keep_ref.shape[2]
    total = in_ref[0].astype(F32)
    for x in range(1, in_ref.shape[0]):
        total += in_ref[x].astype(F32)
    low_u = total[:, units:].astype(BF)
    grad = total[:, :units] + nn(low_u, a_ref[...])
    gate = keep_ref[0] + got_ref[0].astype(F32)
    up = keep_ref[1] + got_ref[1].astype(F32)
    sigma = jax.nn.sigmoid(gate)
    active = gate * sigma
    hidden = (active * up).astype(BF)
    ga_ref[...] = tn(low_u, hidden)
    out_ref[:, :units] = (grad * up * sigma * (1.0 + gate * (1.0 - sigma))).astype(BF)
    low_v = nt(hidden, a_ref[...]).astype(BF)
    out_ref[:, units:] = jnp.concatenate([(grad * active).astype(BF), low_v], axis=1)


def back_kernel(g_ref, h_ref, own_ref, half_ref, out_hbm, v_ref, out_ref, out_sems):
    chips = out_ref.shape[0]
    units = own_ref.shape[2]
    mine = [g_ref[:, i * units : (i + 1) * units] for i in range(2)]
    other = [h_ref[:, i * units : (i + 1) * units] for i in range(2)]
    stores = []
    for x in range(chips):
        term = nn(mine[0], own_ref[0, x]) + nn(mine[1], own_ref[1, x])
        term += nn(other[0], half_ref[0, x]) + nn(other[1], half_ref[1, x])
        out_ref[x] = term.astype(BF)
        stores.append(pltpu.make_async_copy(out_ref.at[x], out_hbm.at[x], out_sems.at[x]))
        stores[x].start()
    v_ref[...] = (g_ref[:, 2 * units :].astype(F32) + h_ref[:, 2 * units :].astype(F32)).astype(BF)
    for store in stores:
        store.wait()


def pick_kernel(ids_ref, *pick_refs):
    rows, count = pick_refs[0].shape
    halves = len(pick_refs)
    each = FLAT * CAP * halves
    row = lax.broadcasted_iota(jnp.int32, (rows, count), 0)
    inner = lax.rem(row, each)
    own = lax.div(row, each) * FLAT + lax.div(inner, CAP * halves)
    hit = jnp.zeros((rows, count), F32)
    for k in range(ids_ref.shape[0]):
        hit = jnp.where(ids_ref[k : k + 1, :] == own, 1.0, hit)
    first = lax.broadcasted_iota(jnp.int32, (count, count), 0)
    second = lax.broadcasted_iota(jnp.int32, (count, count), 1)
    before = jnp.where(first < second, 1.0, 0.0).astype(BF)
    code = jnp.where(hit > 0.5, nn(hit.astype(BF), before), -1.0)
    slot = lax.div(lax.rem(inner, CAP * halves), halves).astype(F32)
    for h, ref in enumerate(pick_refs):
        ref[...] = jnp.where((code == slot) & (lax.rem(row, halves) == h), 1.0, 0.0).astype(BF)


def total_kernel(in_ref, out_hbm, out_ref, sem):
    deep = out_ref.shape[1] // CAP
    for s in range(CAP):
        for y in range(FLAT):
            rows = slice((s * FLAT + y) * deep, (s * FLAT + y + 1) * deep)
            total = in_ref[0, rows].astype(F32)
            for x in range(1, in_ref.shape[0]):
                total += in_ref[x, rows].astype(F32)
            out_ref[y, s * deep : (s + 1) * deep] = total.astype(BF)
    fetch([(out_ref, out_hbm)], sem)


def repack_kernel(in_ref, out_hbm, out_ref, sem):
    rows, width = in_ref.shape
    part = out_ref.shape[1]
    halves = width // part
    each = FLAT * CAP * halves
    deep = out_ref.shape[0] // each
    row = lax.broadcasted_iota(jnp.int32, (out_ref.shape[0], rows), 0)
    there = lax.broadcasted_iota(jnp.int32, (out_ref.shape[0], rows), 1)
    came = lax.div(lax.rem(row, each), halves) * deep + lax.div(row, each)
    total = jnp.zeros(out_ref.shape, F32)
    for h in range(halves):
        move = (there == came) & (lax.rem(row, halves) == h)
        total += nn(jnp.where(move, 1.0, 0.0).astype(BF), in_ref[:, h * part : (h + 1) * part])
    out_ref[...] = total.astype(BF)
    fetch([(out_ref, out_hbm)], sem)


def adapter_kernel(v0_ref, v1_ref, v2_ref, v3_ref, s_ref, o_ref):
    low = v0_ref[...].astype(F32) + v1_ref[...].astype(F32)
    low += v2_ref[...].astype(F32) + v3_ref[...].astype(F32)
    o_ref[...] = tn(low.astype(BF), s_ref[...])


def combine_kernel(*refs):
    *pick_refs, r_ref, o_ref = refs
    part = r_ref.shape[1]
    for h, ref in enumerate(pick_refs):
        o_ref[:, h * part : (h + 1) * part] = tn(ref[...], r_ref[...]).astype(BF)


def call(body, outs, *args, scalars=0, places=(), ends=(), scratch=()):
    vmem = pl.BlockSpec(memory_space=pltpu.VMEM)
    smem = pl.BlockSpec(memory_space=pltpu.SMEM)
    places = places or [vmem] * (len(args) - scalars)
    return pl.pallas_call(
        body,
        out_shape=outs,
        in_specs=[smem] * scalars + list(places),
        out_specs=ends or jax.tree.map(lambda _: vmem, outs),
        scratch_shapes=list(scratch),
        compiler_params=PARAMS,
    )(*args)


def per_device(tokens, grad_out, prob, ids, w_gate, w_up, w_down, adapter_a, adapter_b):
    experts = lax.axis_size(("z", "y"))
    chips = lax.axis_size("x")
    count, width = tokens.shape
    rank = adapter_b.shape[1]
    units = w_gate.shape[1]
    routes = experts * CAP
    w_gate, w_up, w_down, adapter_a, adapter_b = (
        w_gate[0], w_up[0], w_down[0], adapter_a[0], adapter_b[0],
    )
    sds = jax.ShapeDtypeStruct
    me = jnp.stack([lax.axis_index("x"), lax.axis_index("c")]).astype(jnp.int32)

    def swap(block):
        return lax.ppermute(block, "c", [(0, 1), (1, 0)])

    def shift(block, by):
        return lax.ppermute(block, "x", [(i, (i + by) % chips) for i in range(chips)])

    def over_x(block):
        return lax.all_to_all(block, "x", 0, 0, tiled=True)

    def route(block):
        return lax.all_to_all(block, ("y", "z"), 0, 0, tiled=True)

    parts = 2 * width // LANE
    slow = pl.BlockSpec(memory_space=pltpu.HBM)

    def pin(*arrays):
        return [pltpu.with_memory_space_constraint(x, pltpu.HBM) for x in arrays]

    near = pl.BlockSpec(memory_space=pltpu.VMEM)
    far = pl.BlockSpec(memory_space=pltpu.HBM)
    dma = pltpu.SemaphoreType.DMA

    packed = call(
        pack_kernel, sds((experts * parts, CAP * LANE), BF),
        *pin(ids.T, prob.T, tokens, grad_out),
        places=[slow] * 4,
        scratch=[
            pltpu.VMEM(ids.T.shape, ids.dtype), pltpu.VMEM(prob.T.shape, F32),
            pltpu.VMEM(tokens.shape, BF), pltpu.VMEM(tokens.shape, BF), dma((4,)),
        ],
    )
    arrived = route(packed.reshape(experts, parts, CAP * LANE))

    own_cols, half, *down = call(
        prep_kernel,
        (sds((2, chips, units, width), BF),) * 2 + (sds((units, 2 * width), BF),) * 4,
        me, w_gate, w_up, w_down, scalars=1,
    )
    half = swap(half)
    down = down[:1] + [shift(block, d + 1) for d, block in enumerate(down[1:])]
    b_other = swap(adapter_b)
    arrived, half, b_other, *down = lax.optimization_barrier((arrived, half, b_other, *down))

    x_four, s_own = call(
        split_kernel, (pltpu.HBM((chips, routes, width), BF), pltpu.HBM((routes, width), BF)),
        arrived.reshape(experts * parts, CAP * LANE),
        ends=(far, far),
        scratch=[pltpu.VMEM((routes, width), BF)] * 2 + [dma((chips + 1,))],
    )
    x_all = over_x(x_four)
    s_other = swap(s_own)
    shares = (chips, routes, units + rank)
    sources = (s_own, s_other, adapter_b, b_other, *down)
    part = call(
        part_kernel, pltpu.HBM(shares, BF), me, *pin(*sources), scalars=1,
        places=[slow] * len(sources), ends=far,
        scratch=[pltpu.VMEM(x.shape, BF) for x in (*sources, sds(shares, BF))] + [dma((len(sources),))],
    )
    sums = over_x(part)
    keep, send = call(
        gate_kernel,
        (pltpu.HBM((2, routes, units), F32), sds((2, routes, units), BF)),
        x_all, own_cols, half, ends=(far, near),
        scratch=[pltpu.VMEM((2, routes, units), F32), dma((1,))],
    )
    got = swap(send)
    sources = (keep, got, sums, adapter_a)
    grads, grad_a = call(
        grad_kernel,
        (sds((routes, 2 * units + rank), BF), sds((rank, units), F32)),
        *pin(*sources), places=[slow] * 4,
        scratch=[pltpu.VMEM(x.shape, x.dtype) for x in sources] + [dma((4,))],
    )
    grads_other = swap(grads)
    back_shape = (chips, routes, width)
    back, v_pair = call(
        back_kernel, (pltpu.HBM(back_shape, BF), sds((routes, rank), BF)),
        grads, grads_other, own_cols, half, ends=(far, near),
        scratch=[pltpu.VMEM(back_shape, BF), dma((chips,))],
    )
    halves, deep = 2, experts // FLAT
    each = FLAT * CAP * halves
    picks = call(pick_kernel, (sds((deep * each, count), BF),) * halves, ids.T)
    backs, *picks = lax.optimization_barrier((over_x(back), *picks))
    shape = (FLAT, CAP * deep, width)
    total = call(
        total_kernel, pltpu.HBM(shape, BF), backs, ends=far, scratch=[pltpu.VMEM(shape, BF), dma((1,))]
    )
    near_home = lax.all_to_all(total, "y", 0, 0, tiled=True)
    shape = (deep * each, width // halves)
    ready = call(
        repack_kernel, pltpu.HBM(shape, BF), near_home.reshape(routes, width), ends=far,
        scratch=[pltpu.VMEM(shape, BF), dma((1,))],
    )
    ready, v_pair = lax.optimization_barrier((ready, v_pair))
    home = lax.all_to_all(ready.reshape(deep, each, width // halves), "z", 0, 0, tiled=True)

    v_all = [v_pair] + [shift(v_pair, d) for d in (1, 2, 3)]
    grad_b = call(adapter_kernel, sds((rank, width), F32), *v_all, s_own)
    out = call(combine_kernel, sds(tokens.shape, BF), *picks, home.reshape(shape))
    return out, grad_a[None], grad_b[None]


def solution(mesh):
    fine = Mesh(mesh.devices.reshape(4, 2, 16, 4), ("x", "c", "z", "y"))
    dp, ex = ("x", "c"), ("z", "y")
    specs = (
        P(ex, dp), P(ex, dp), P(ex, None), P(ex, None),
        P(ex, dp, None), P(ex, dp, None), P(ex, dp, None), P(ex, None, dp), P(ex, None, dp),
    )
    return jax.shard_map(
        per_device,
        mesh=fine,
        in_specs=specs,
        out_specs=(P(ex, dp), P(ex, None, dp), P(ex, None, dp)),
        check_vma=False,
    )
```

```python
import jax
import jax.numpy as jnp
from jax import lax
from jax.experimental import pallas as pl
from jax.experimental.pallas import tpu as pltpu
from jax.sharding import Mesh, PartitionSpec as P

CAP = 5
BF = jnp.bfloat16
F32 = jnp.float32
LANE = 128
FLAT = 4
PARAMS = pltpu.CompilerParams(vmem_limit_bytes=16 * 1024 * 1024)


def nt(left, right):
    return lax.dot_general(left, right, (((1,), (1,)), ((), ())), preferred_element_type=F32)


def tn(left, right):
    return lax.dot_general(left, right, (((0,), (0,)), ((), ())), preferred_element_type=F32)


def nn(left, right):
    return jnp.dot(left, right, preferred_element_type=F32)


def lanes(index, width):
    return pl.ds(pl.multiple_of(index * width, width), width)


def fetch(pairs, sems):
    copies = [pltpu.make_async_copy(src, dst, sems.at[i]) for i, (src, dst) in enumerate(pairs)]
    for copy in copies:
        copy.start()
    for copy in copies:
        copy.wait()


def low(value, size):
    return value & (size - 1)


def high(value, size):
    return value >> (size.bit_length() - 1)


def expert_of(place):
    outer, inner = high(place, FLAT * FLAT), low(place, FLAT * FLAT)
    return low(inner, FLAT) * (FLAT * FLAT) + outer * FLAT + high(inner, FLAT)


def pack_kernel(ids_hbm, prob_hbm, tok_hbm, dy_hbm, out_ref, ids_ref, prob_ref, tok_ref, dy_ref, sems):
    fetch(
        [(ids_hbm, ids_ref), (prob_hbm, prob_ref), (tok_hbm, tok_ref), (dy_hbm, dy_ref)], sems
    )
    rows = out_ref.shape[0]
    count, width = tok_ref.shape
    parts = 2 * width // LANE
    span = parts * count
    row = lax.broadcasted_iota(jnp.int32, (rows, count), 0)
    own = expert_of(high(row, parts))
    hit = jnp.zeros((rows, count), F32)
    weight = jnp.zeros((rows, count), F32)
    for k in range(ids_ref.shape[0]):
        same = ids_ref[k : k + 1, :] == own
        hit = jnp.where(same, 1.0, hit)
        weight = jnp.where(same, prob_ref[k : k + 1, :], weight)
    weight = jnp.where(low(row, parts) < parts // 2, hit, weight)
    first = lax.broadcasted_iota(jnp.int32, (count, count), 0)
    second = lax.broadcasted_iota(jnp.int32, (count, count), 1)
    before = jnp.where(first < second, 1.0, 0.0).astype(BF)
    code = jnp.where(hit > 0.5, nn(hit.astype(BF), before), -1.0)
    wide_row = lax.broadcasted_iota(jnp.int32, (rows, span), 0)
    lane = lax.broadcasted_iota(jnp.int32, (rows, span), 1)
    here = low(wide_row, parts) == high(lane, count)
    spread = jnp.where(here, jnp.concatenate([code] * parts, axis=1), -1.0)
    table = jnp.concatenate(
        [ref[:, c : c + LANE] for ref in (tok_ref, dy_ref) for c in range(0, width, LANE)], axis=0
    )
    for s in range(CAP):
        pick = jnp.where(spread == float(s), 1.0, 0.0).astype(BF)
        scale = jnp.sum(jnp.where(code == float(s), weight, 0.0), axis=1, keepdims=True)
        out_ref[:, s * LANE : (s + 1) * LANE] = (nn(pick, table) * scale).astype(BF)


def code_of(ids, experts):
    count = ids.shape[1]
    own = expert_of(lax.broadcasted_iota(jnp.int32, (experts, count), 0))
    hit = jnp.zeros((experts, count), F32)
    for k in range(ids.shape[0]):
        hit = jnp.where(ids[k : k + 1, :] == own, 1.0, hit)
    first = lax.broadcasted_iota(jnp.int32, (count, count), 0)
    second = lax.broadcasted_iota(jnp.int32, (count, count), 1)
    before = jnp.where(first < second, 1.0, 0.0).astype(BF)
    return jnp.where(hit > 0.5, nn(hit.astype(BF), before), -1.0)


def split_kernel(in_ref, x_hbm, s_hbm, x_ref, s_ref, sems):
    total = in_ref.shape[0]
    width = s_ref.shape[1]
    parts = 2 * width // LANE
    experts = total // parts
    first = lax.broadcasted_iota(jnp.int32, (total, total), 0)
    second = lax.broadcasted_iota(jnp.int32, (total, total), 1)
    there = low(first, experts) * parts + high(first, experts)
    perm = jnp.where(second == there, 1.0, 0.0).astype(BF)
    rows = nn(perm, in_ref[...]).astype(BF)
    for r in range(parts):
        ref = x_ref if r < parts // 2 else s_ref
        at = (r % (parts // 2)) * LANE
        for s in range(CAP):
            ref[s * experts : (s + 1) * experts, at : at + LANE] = rows[
                r * experts : (r + 1) * experts, s * LANE : (s + 1) * LANE
            ]
    chips = x_hbm.shape[0]
    fetch([(x_ref, x_hbm.at[x]) for x in range(chips)] + [(s_ref, s_hbm)], sems)


def prep_kernel(me_ref, wg_ref, wu_ref, wd_ref, own_ref, swap_ref, d0_ref, d1_ref, d2_ref, d3_ref):
    chip, core = me_ref[0], me_ref[1]
    chips, units, width = swap_ref.shape[1:]
    for d, ref in enumerate((d0_ref, d1_ref, d2_ref, d3_ref)):
        ref[...] = wd_ref[:, lanes(lax.rem(chip + d, chips), 2 * width)]
    for x in range(chips):
        for ref, which in ((own_ref, core), (swap_ref, 1 - core)):
            cols = lanes(2 * x + which, width)
            ref[0, x] = wg_ref[:, cols]
            ref[1, x] = wu_ref[:, cols]


def part_kernel(me_ref, *refs):
    chip, core = me_ref[0], me_ref[1]
    sources, out_hbm, held, out_ref, sems = refs[:8], refs[8], refs[9:17], refs[17], refs[18]
    fetch(list(zip(sources, held)), sems)
    s_ref, t_ref, b_ref, o_ref = held[:4]
    units, width = held[4].shape[0], s_ref.shape[1]
    chips = out_ref.shape[0]
    mine, other = s_ref[...], t_ref[...]
    low = (nt(mine, b_ref[...]) + nt(other, o_ref[...])).astype(BF)
    for d, ref in enumerate(held[4:]):
        w_mine, w_other = ref[:, lanes(core, width)], ref[:, lanes(1 - core, width)]
        to = lax.rem(chip + chips - d, chips)
        out_ref[to, :, :units] = (nt(mine, w_mine) + nt(other, w_other)).astype(BF)
        out_ref[to, :, units:] = low
    fetch([(out_ref, out_hbm)], sems)


def gate_kernel(x_ref, own_ref, half_ref, keep_hbm, send_ref, keep_ref, sem):
    chips, routes, width = x_ref.shape
    units = own_ref.shape[2]
    keep = [jnp.zeros((routes, units), F32)] * 2
    send = [jnp.zeros((routes, units), F32)] * 2
    for x in range(chips):
        for i in range(2):
            keep[i] = keep[i] + nt(x_ref[x], own_ref[i, x])
    for i in range(2):
        keep_ref[i] = keep[i]
    store = pltpu.make_async_copy(keep_ref, keep_hbm, sem.at[0])
    store.start()
    for x in range(chips):
        for i in range(2):
            send[i] = send[i] + nt(x_ref[x], half_ref[i, x])
    for i in range(2):
        send_ref[i] = send[i].astype(BF)
    store.wait()


def grad_kernel(keep_hbm, got_hbm, in_hbm, a_hbm, out_ref, ga_ref, keep_ref, got_ref, in_ref, a_ref, sems):
    fetch([(keep_hbm, keep_ref), (got_hbm, got_ref), (in_hbm, in_ref), (a_hbm, a_ref)], sems)
    units = keep_ref.shape[2]
    total = in_ref[0].astype(F32)
    for x in range(1, in_ref.shape[0]):
        total += in_ref[x].astype(F32)
    low_u = total[:, units:].astype(BF)
    grad = total[:, :units] + nn(low_u, a_ref[...])
    gate = keep_ref[0] + got_ref[0].astype(F32)
    up = keep_ref[1] + got_ref[1].astype(F32)
    sigma = jax.nn.sigmoid(gate)
    active = gate * sigma
    hidden = (active * up).astype(BF)
    ga_ref[...] = tn(low_u, hidden)
    out_ref[:, :units] = (grad * up * sigma * (1.0 + gate * (1.0 - sigma))).astype(BF)
    low_v = nt(hidden, a_ref[...]).astype(BF)
    out_ref[:, units:] = jnp.concatenate([(grad * active).astype(BF), low_v], axis=1)


def back_kernel(g_ref, h_ref, own_ref, half_ref, out_hbm, v_ref, out_ref, out_sems):
    chips = out_ref.shape[0]
    units = own_ref.shape[2]
    mine = [g_ref[:, i * units : (i + 1) * units] for i in range(2)]
    other = [h_ref[:, i * units : (i + 1) * units] for i in range(2)]
    stores = []
    for x in range(chips):
        term = nn(mine[0], own_ref[0, x]) + nn(mine[1], own_ref[1, x])
        term += nn(other[0], half_ref[0, x]) + nn(other[1], half_ref[1, x])
        out_ref[x] = term.astype(BF)
        stores.append(pltpu.make_async_copy(out_ref.at[x], out_hbm.at[x], out_sems.at[x]))
        stores[x].start()
    v_ref[...] = (g_ref[:, 2 * units :].astype(F32) + h_ref[:, 2 * units :].astype(F32)).astype(BF)
    for store in stores:
        store.wait()


def code_kernel(ids_ref, code_ref):
    code_ref[...] = code_of(ids_ref[...], code_ref.shape[0])


def total_kernel(in_ref, out_ref):
    experts = out_ref.shape[0]
    width = in_ref.shape[2]
    for s in range(CAP):
        rows = slice(s * experts, (s + 1) * experts)
        total = in_ref[0, rows].astype(F32)
        for x in range(1, in_ref.shape[0]):
            total += in_ref[x, rows].astype(F32)
        out_ref[:, s * width : (s + 1) * width] = total.astype(BF)


def adapter_kernel(v0_ref, v1_ref, v2_ref, v3_ref, s_ref, o_ref):
    low = v0_ref[...].astype(F32) + v1_ref[...].astype(F32)
    low += v2_ref[...].astype(F32) + v3_ref[...].astype(F32)
    o_ref[...] = tn(low.astype(BF), s_ref[...])


def combine_kernel(code_ref, r_ref, o_ref):
    width = o_ref.shape[1]
    total = jnp.zeros(o_ref.shape, F32)
    for s in range(CAP):
        pick = jnp.where(code_ref[...] == float(s), 1.0, 0.0).astype(BF)
        total += tn(pick, r_ref[:, s * width : (s + 1) * width])
    o_ref[...] = total.astype(BF)


def call(body, outs, *args, scalars=0, places=(), ends=(), scratch=()):
    vmem = pl.BlockSpec(memory_space=pltpu.VMEM)
    smem = pl.BlockSpec(memory_space=pltpu.SMEM)
    places = places or [vmem] * (len(args) - scalars)
    return pl.pallas_call(
        body,
        out_shape=outs,
        in_specs=[smem] * scalars + list(places),
        out_specs=ends or jax.tree.map(lambda _: vmem, outs),
        scratch_shapes=list(scratch),
        compiler_params=PARAMS,
    )(*args)


def per_device(tokens, grad_out, prob, ids, w_gate, w_up, w_down, adapter_a, adapter_b):
    experts = lax.axis_size(("zh", "zl", "y"))
    chips = lax.axis_size("x")
    count, width = tokens.shape
    rank = adapter_b.shape[1]
    units = w_gate.shape[1]
    routes = experts * CAP
    w_gate, w_up, w_down, adapter_a, adapter_b = (
        w_gate[0], w_up[0], w_down[0], adapter_a[0], adapter_b[0],
    )
    sds = jax.ShapeDtypeStruct
    me = jnp.stack([lax.axis_index("x"), lax.axis_index("c")]).astype(jnp.int32)

    def swap(block):
        return lax.ppermute(block, "c", [(0, 1), (1, 0)])

    def shift(block, by):
        return lax.ppermute(block, "x", [(i, (i + by) % chips) for i in range(chips)])

    def over_x(block):
        return lax.all_to_all(block, "x", 0, 0, tiled=True)

    def route(block):
        return lax.all_to_all(block, ("zl", "y", "zh"), 0, 0, tiled=True)

    parts = 2 * width // LANE
    slow = pl.BlockSpec(memory_space=pltpu.HBM)

    def pin(*arrays):
        return [pltpu.with_memory_space_constraint(x, pltpu.HBM) for x in arrays]

    near = pl.BlockSpec(memory_space=pltpu.VMEM)
    far = pl.BlockSpec(memory_space=pltpu.HBM)
    dma = pltpu.SemaphoreType.DMA

    packed = call(
        pack_kernel, sds((experts * parts, CAP * LANE), BF),
        *pin(ids.T, prob.T, tokens, grad_out),
        places=[slow] * 4,
        scratch=[
            pltpu.VMEM(ids.T.shape, ids.dtype), pltpu.VMEM(prob.T.shape, F32),
            pltpu.VMEM(tokens.shape, BF), pltpu.VMEM(tokens.shape, BF), dma((4,)),
        ],
    )
    arrived = route(packed.reshape(experts, parts, CAP * LANE))

    own_cols, half, *down = call(
        prep_kernel,
        (sds((2, chips, units, width), BF),) * 2 + (sds((units, 2 * width), BF),) * 4,
        me, w_gate, w_up, w_down, scalars=1,
    )
    half = swap(half)
    down = down[:1] + [shift(block, d + 1) for d, block in enumerate(down[1:])]
    b_other = swap(adapter_b)
    arrived, half, b_other, *down = lax.optimization_barrier((arrived, half, b_other, *down))

    x_four, s_own = call(
        split_kernel, (pltpu.HBM((chips, routes, width), BF), pltpu.HBM((routes, width), BF)),
        arrived.reshape(experts * parts, CAP * LANE),
        ends=(far, far),
        scratch=[pltpu.VMEM((routes, width), BF)] * 2 + [dma((chips + 1,))],
    )
    x_all = over_x(x_four)
    s_other = swap(s_own)
    shares = (chips, routes, units + rank)
    sources = (s_own, s_other, adapter_b, b_other, *down)
    part = call(
        part_kernel, pltpu.HBM(shares, BF), me, *pin(*sources), scalars=1,
        places=[slow] * len(sources), ends=far,
        scratch=[pltpu.VMEM(x.shape, BF) for x in (*sources, sds(shares, BF))] + [dma((len(sources),))],
    )
    sums = over_x(part)
    keep, send = call(
        gate_kernel,
        (pltpu.HBM((2, routes, units), F32), sds((2, routes, units), BF)),
        x_all, own_cols, half, ends=(far, near),
        scratch=[pltpu.VMEM((2, routes, units), F32), dma((1,))],
    )
    got = swap(send)
    sources = (keep, got, sums, adapter_a)
    grads, grad_a = call(
        grad_kernel,
        (sds((routes, 2 * units + rank), BF), sds((rank, units), F32)),
        *pin(*sources), places=[slow] * 4,
        scratch=[pltpu.VMEM(x.shape, x.dtype) for x in sources] + [dma((4,))],
    )
    grads_other = swap(grads)
    back_shape = (chips, routes, width)
    back, v_pair = call(
        back_kernel, (pltpu.HBM(back_shape, BF), sds((routes, rank), BF)),
        grads, grads_other, own_cols, half, ends=(far, near),
        scratch=[pltpu.VMEM(back_shape, BF), dma((chips,))],
    )
    code = call(code_kernel, sds((experts, count), F32), ids.T)
    backs, code = lax.optimization_barrier((over_x(back), code))
    total = call(total_kernel, sds((experts, CAP * width), BF), backs)
    home = route(total.reshape(experts, 2, CAP * width // 2)).reshape(experts, CAP * width)

    v_all = [v_pair] + [shift(v_pair, d) for d in (1, 2, 3)]
    grad_b = call(adapter_kernel, sds((rank, width), F32), *v_all, s_own)
    out = call(combine_kernel, sds(tokens.shape, BF), code, home)
    return out, grad_a[None], grad_b[None]


def solution(mesh):
    fine = Mesh(mesh.devices.reshape(4, 2, 4, 4, 4), ("x", "c", "zh", "zl", "y"))
    dp, ex = ("x", "c"), ("zh", "zl", "y")
    specs = (
        P(ex, dp), P(ex, dp), P(ex, None), P(ex, None),
        P(ex, dp, None), P(ex, dp, None), P(ex, dp, None), P(ex, None, dp), P(ex, None, dp),
    )
    return jax.shard_map(
        per_device,
        mesh=fine,
        in_specs=specs,
        out_specs=(P(ex, dp), P(ex, None, dp), P(ex, None, dp)),
        check_vma=False,
    )
```

```python
import jax
import jax.numpy as jnp
from jax import lax
from jax.experimental import pallas as pl
from jax.experimental.pallas import tpu as pltpu
from jax.sharding import Mesh, PartitionSpec as P

CAP = 5
BF = jnp.bfloat16
F32 = jnp.float32
LANE = 128
FLAT = 4


def nt(left, right):
    return lax.dot_general(left, right, (((1,), (1,)), ((), ())), preferred_element_type=F32)


def tn(left, right):
    return lax.dot_general(left, right, (((0,), (0,)), ((), ())), preferred_element_type=F32)


def nn(left, right):
    return jnp.dot(left, right, preferred_element_type=F32)


def lanes(index, width):
    return pl.ds(pl.multiple_of(index * width, width), width)


def fetch(pairs, sems):
    copies = [pltpu.make_async_copy(src, dst, sems.at[i]) for i, (src, dst) in enumerate(pairs)]
    for copy in copies:
        copy.start()
    for copy in copies:
        copy.wait()


def low(value, size):
    return value & (size - 1)


def high(value, size):
    return value >> (size.bit_length() - 1)


def expert_of(place):
    outer, inner = high(place, FLAT * FLAT), low(place, FLAT * FLAT)
    return low(inner, FLAT) * (FLAT * FLAT) + outer * FLAT + high(inner, FLAT)


def pack_kernel(ids_hbm, prob_hbm, tok_hbm, dy_hbm, out_ref, ids_ref, prob_ref, tok_ref, dy_ref, sems):
    fetch(
        [(ids_hbm, ids_ref), (prob_hbm, prob_ref), (tok_hbm, tok_ref), (dy_hbm, dy_ref)], sems
    )
    rows = out_ref.shape[0]
    count, width = tok_ref.shape
    parts = 2 * width // LANE
    span = parts * count
    row = lax.broadcasted_iota(jnp.int32, (rows, count), 0)
    own = expert_of(high(row, parts))
    hit = jnp.zeros((rows, count), F32)
    weight = jnp.zeros((rows, count), F32)
    for k in range(ids_ref.shape[0]):
        same = ids_ref[k : k + 1, :] == own
        hit = jnp.where(same, 1.0, hit)
        weight = jnp.where(same, prob_ref[k : k + 1, :], weight)
    weight = jnp.where(low(row, parts) < parts // 2, hit, weight)
    first = lax.broadcasted_iota(jnp.int32, (count, count), 0)
    second = lax.broadcasted_iota(jnp.int32, (count, count), 1)
    before = jnp.where(first < second, 1.0, 0.0).astype(BF)
    code = jnp.where(hit > 0.5, nn(hit.astype(BF), before), -1.0)
    wide_row = lax.broadcasted_iota(jnp.int32, (rows, span), 0)
    lane = lax.broadcasted_iota(jnp.int32, (rows, span), 1)
    here = low(wide_row, parts) == high(lane, count)
    spread = jnp.where(here, jnp.concatenate([code] * parts, axis=1), -1.0)
    table = jnp.concatenate(
        [ref[:, c : c + LANE] for ref in (tok_ref, dy_ref) for c in range(0, width, LANE)], axis=0
    )
    for s in range(CAP):
        pick = jnp.where(spread == float(s), 1.0, 0.0).astype(BF)
        scale = jnp.sum(jnp.where(code == float(s), weight, 0.0), axis=1, keepdims=True)
        out_ref[:, s * LANE : (s + 1) * LANE] = (nn(pick, table) * scale).astype(BF)


def code_of(ids, experts):
    count = ids.shape[1]
    own = expert_of(lax.broadcasted_iota(jnp.int32, (experts, count), 0))
    hit = jnp.zeros((experts, count), F32)
    for k in range(ids.shape[0]):
        hit = jnp.where(ids[k : k + 1, :] == own, 1.0, hit)
    first = lax.broadcasted_iota(jnp.int32, (count, count), 0)
    second = lax.broadcasted_iota(jnp.int32, (count, count), 1)
    before = jnp.where(first < second, 1.0, 0.0).astype(BF)
    return jnp.where(hit > 0.5, nn(hit.astype(BF), before), -1.0)


def split_kernel(in_hbm, x_hbm, s_hbm, in_ref, x_ref, s_ref, sems):
    load = pltpu.make_async_copy(in_hbm, in_ref, sems.at[0])
    load.start()
    total = in_ref.shape[0]
    width = s_ref.shape[1]
    parts = 2 * width // LANE
    experts = total // parts
    first = lax.broadcasted_iota(jnp.int32, (total, total), 0)
    second = lax.broadcasted_iota(jnp.int32, (total, total), 1)
    there = low(first, experts) * parts + high(first, experts)
    perm = jnp.where(second == there, 1.0, 0.0).astype(BF)
    load.wait()
    rows = nn(perm, in_ref[...]).astype(BF)
    for r in range(parts):
        ref = x_ref if r < parts // 2 else s_ref
        at = (r % (parts // 2)) * LANE
        for s in range(CAP):
            ref[s * experts : (s + 1) * experts, at : at + LANE] = rows[
                r * experts : (r + 1) * experts, s * LANE : (s + 1) * LANE
            ]
    chips = x_hbm.shape[0]
    fetch([(x_ref, x_hbm.at[x]) for x in range(chips)] + [(s_ref, s_hbm)], sems)


def prep_kernel(me_ref, wg_ref, wu_ref, wd_ref, own_ref, swap_ref, d0_ref, d1_ref, d2_ref, d3_ref):
    chip, core = me_ref[0], me_ref[1]
    chips, units, width = swap_ref.shape[1:]
    for d, ref in enumerate((d0_ref, d1_ref, d2_ref, d3_ref)):
        ref[...] = wd_ref[:, lanes(lax.rem(chip + d, chips), 2 * width)]
    for x in range(chips):
        for ref, which in ((own_ref, core), (swap_ref, 1 - core)):
            cols = lanes(2 * x + which, width)
            ref[0, x] = wg_ref[:, cols]
            ref[1, x] = wu_ref[:, cols]


def part_kernel(me_ref, *refs):
    chip, core = me_ref[0], me_ref[1]
    sources, out_hbm, held, out_ref, sems = refs[:8], refs[8], refs[9:17], refs[17], refs[18]
    fetch(list(zip(sources, held)), sems)
    s_ref, t_ref, b_ref, o_ref = held[:4]
    units, width = held[4].shape[0], s_ref.shape[1]
    chips = out_ref.shape[0]
    mine, other = s_ref[...], t_ref[...]
    low = (nt(mine, b_ref[...]) + nt(other, o_ref[...])).astype(BF)
    for d, ref in enumerate(held[4:]):
        w_mine, w_other = ref[:, lanes(core, width)], ref[:, lanes(1 - core, width)]
        to = lax.rem(chip + chips - d, chips)
        out_ref[to, :, :units] = (nt(mine, w_mine) + nt(other, w_other)).astype(BF)
        out_ref[to, :, units:] = low
    fetch([(out_ref, out_hbm)], sems)


def gate_kernel(x_ref, own_ref, half_ref, keep_hbm, send_ref, keep_ref, sem):
    chips, routes, width = x_ref.shape
    units = own_ref.shape[2]
    keep = [jnp.zeros((routes, units), F32)] * 2
    send = [jnp.zeros((routes, units), F32)] * 2
    for x in range(chips):
        for i in range(2):
            keep[i] = keep[i] + nt(x_ref[x], own_ref[i, x])
    for i in range(2):
        keep_ref[i] = keep[i]
    store = pltpu.make_async_copy(keep_ref, keep_hbm, sem.at[0])
    store.start()
    for x in range(chips):
        for i in range(2):
            send[i] = send[i] + nt(x_ref[x], half_ref[i, x])
    for i in range(2):
        send_ref[i] = send[i].astype(BF)
    store.wait()


def grad_kernel(keep_hbm, got_hbm, in_hbm, a_hbm, out_ref, ga_ref, keep_ref, got_ref, in_ref, a_ref, sems):
    fetch([(keep_hbm, keep_ref), (got_hbm, got_ref), (in_hbm, in_ref), (a_hbm, a_ref)], sems)
    units = keep_ref.shape[2]
    total = in_ref[0].astype(F32)
    for x in range(1, in_ref.shape[0]):
        total += in_ref[x].astype(F32)
    low_u = total[:, units:].astype(BF)
    grad = total[:, :units] + nn(low_u, a_ref[...])
    gate = keep_ref[0] + got_ref[0].astype(F32)
    up = keep_ref[1] + got_ref[1].astype(F32)
    sigma = jax.nn.sigmoid(gate)
    active = gate * sigma
    hidden = (active * up).astype(BF)
    ga_ref[...] = tn(low_u, hidden)
    out_ref[:, :units] = (grad * up * sigma * (1.0 + gate * (1.0 - sigma))).astype(BF)
    low_v = nt(hidden, a_ref[...]).astype(BF)
    out_ref[:, units:] = jnp.concatenate([(grad * active).astype(BF), low_v], axis=1)


def back_kernel(g_ref, h_ref, own_ref, half_ref, out_hbm, v_ref, out_ref, out_sems):
    chips = out_ref.shape[0]
    units = own_ref.shape[2]
    mine = [g_ref[:, i * units : (i + 1) * units] for i in range(2)]
    other = [h_ref[:, i * units : (i + 1) * units] for i in range(2)]
    stores = []
    for x in range(chips):
        term = nn(mine[0], own_ref[0, x]) + nn(mine[1], own_ref[1, x])
        term += nn(other[0], half_ref[0, x]) + nn(other[1], half_ref[1, x])
        out_ref[x] = term.astype(BF)
        stores.append(pltpu.make_async_copy(out_ref.at[x], out_hbm.at[x], out_sems.at[x]))
        stores[x].start()
    v_ref[...] = (g_ref[:, 2 * units :].astype(F32) + h_ref[:, 2 * units :].astype(F32)).astype(BF)
    for store in stores:
        store.wait()


def code_kernel(ids_ref, code_ref):
    code_ref[...] = code_of(ids_ref[...], code_ref.shape[0])


def total_kernel(in_ref, out_ref):
    experts = out_ref.shape[0]
    width = in_ref.shape[2]
    for s in range(CAP):
        rows = slice(s * experts, (s + 1) * experts)
        total = in_ref[0, rows].astype(F32)
        for x in range(1, in_ref.shape[0]):
            total += in_ref[x, rows].astype(F32)
        out_ref[:, s * width : (s + 1) * width] = total.astype(BF)


def adapter_kernel(v0_ref, v1_ref, v2_ref, v3_ref, s_ref, o_ref):
    low = v0_ref[...].astype(F32) + v1_ref[...].astype(F32)
    low += v2_ref[...].astype(F32) + v3_ref[...].astype(F32)
    o_ref[...] = tn(low.astype(BF), s_ref[...])


def combine_kernel(code_ref, r_ref, o_ref):
    width = o_ref.shape[1]
    total = jnp.zeros(o_ref.shape, F32)
    for s in range(CAP):
        pick = jnp.where(code_ref[...] == float(s), 1.0, 0.0).astype(BF)
        total += tn(pick, r_ref[:, s * width : (s + 1) * width])
    o_ref[...] = total.astype(BF)


def call(body, outs, *args, scalars=0, places=(), ends=(), scratch=(), vmem_mib=16):
    vmem = pl.BlockSpec(memory_space=pltpu.VMEM)
    smem = pl.BlockSpec(memory_space=pltpu.SMEM)
    places = places or [vmem] * (len(args) - scalars)
    return pl.pallas_call(
        body,
        out_shape=outs,
        in_specs=[smem] * scalars + list(places),
        out_specs=ends or jax.tree.map(lambda _: vmem, outs),
        scratch_shapes=list(scratch),
        compiler_params=pltpu.CompilerParams(vmem_limit_bytes=vmem_mib * 1024 * 1024),
    )(*args)


def per_device(tokens, grad_out, prob, ids, w_gate, w_up, w_down, adapter_a, adapter_b):
    experts = lax.axis_size(("zh", "zl", "y"))
    chips = lax.axis_size("x")
    count, width = tokens.shape
    rank = adapter_b.shape[1]
    units = w_gate.shape[1]
    routes = experts * CAP
    w_gate, w_up, w_down, adapter_a, adapter_b = (
        w_gate[0], w_up[0], w_down[0], adapter_a[0], adapter_b[0],
    )
    sds = jax.ShapeDtypeStruct
    me = jnp.stack([lax.axis_index("x"), lax.axis_index("c")]).astype(jnp.int32)

    def swap(block):
        return lax.ppermute(block, "c", [(0, 1), (1, 0)])

    def shift(block, by):
        return lax.ppermute(block, "x", [(i, (i + by) % chips) for i in range(chips)])

    def over_x(block):
        return lax.all_to_all(block, "x", 0, 0, tiled=True)

    def route(block):
        return lax.all_to_all(block, ("zl", "y", "zh"), 0, 0, tiled=True)

    parts = 2 * width // LANE
    slow = pl.BlockSpec(memory_space=pltpu.HBM)

    def pin(*arrays):
        return [pltpu.with_memory_space_constraint(x, pltpu.HBM) for x in arrays]

    near = pl.BlockSpec(memory_space=pltpu.VMEM)
    far = pl.BlockSpec(memory_space=pltpu.HBM)
    dma = pltpu.SemaphoreType.DMA

    packed = call(
        pack_kernel, sds((experts * parts, CAP * LANE), BF),
        *pin(ids.T, prob.T, tokens, grad_out),
        places=[slow] * 4,
        scratch=[
            pltpu.VMEM(ids.T.shape, ids.dtype), pltpu.VMEM(prob.T.shape, F32),
            pltpu.VMEM(tokens.shape, BF), pltpu.VMEM(tokens.shape, BF), dma((4,)),
        ],
    )
    arrived = route(packed.reshape(experts, parts, CAP * LANE))

    own_cols, half, *down = call(
        prep_kernel,
        (sds((2, chips, units, width), BF),) * 2 + (sds((units, 2 * width), BF),) * 4,
        me, w_gate, w_up, w_down, scalars=1,
    )
    half = swap(half)
    down = down[:1] + [shift(block, d + 1) for d, block in enumerate(down[1:])]
    b_other = swap(adapter_b)
    arrived, half, b_other, *down = lax.optimization_barrier((arrived, half, b_other, *down))

    x_four, s_own = call(
        split_kernel, (pltpu.HBM((chips, routes, width), BF), pltpu.HBM((routes, width), BF)),
        *pin(arrived.reshape(experts * parts, CAP * LANE)), places=[slow], ends=(far, far),
        scratch=[
            pltpu.VMEM((experts * parts, CAP * LANE), BF), pltpu.VMEM((routes, width), BF),
            pltpu.VMEM((routes, width), BF), dma((chips + 1,)),
        ],
    )
    x_all = over_x(x_four)
    s_other = swap(s_own)
    shares = (chips, routes, units + rank)
    sources = (s_own, s_other, adapter_b, b_other, *down)
    part = call(
        part_kernel, pltpu.HBM(shares, BF), me, *pin(*sources), scalars=1,
        places=[slow] * len(sources), ends=far,
        scratch=[pltpu.VMEM(x.shape, BF) for x in (*sources, sds(shares, BF))] + [dma((len(sources),))],
    )
    sums = over_x(part)
    keep, send = call(
        gate_kernel,
        (pltpu.HBM((2, routes, units), F32), sds((2, routes, units), BF)),
        x_all, own_cols, half, ends=(far, near),
        scratch=[pltpu.VMEM((2, routes, units), F32), dma((1,))],
    )
    got = swap(send)
    sources = (keep, got, sums, adapter_a)
    grads, grad_a = call(
        grad_kernel,
        (sds((routes, 2 * units + rank), BF), sds((rank, units), F32)),
        *pin(*sources), places=[slow] * 4,
        scratch=[pltpu.VMEM(x.shape, x.dtype) for x in sources] + [dma((4,))],
    )
    grads_other = swap(grads)
    back_shape = (chips, routes, width)
    back, v_pair = call(
        back_kernel, (pltpu.HBM(back_shape, BF), sds((routes, rank), BF)),
        grads, grads_other, own_cols, half, ends=(far, near),
        scratch=[pltpu.VMEM(back_shape, BF), dma((chips,))],
    )
    code = call(code_kernel, sds((experts, count), F32), ids.T)
    backs, code = lax.optimization_barrier((over_x(back), code))
    total = call(total_kernel, sds((experts, CAP * width), BF), backs, vmem_mib=63)
    home = route(total.reshape(experts, 2, CAP * width // 2)).reshape(experts, CAP * width)

    v_all = [v_pair] + [shift(v_pair, d) for d in (1, 2, 3)]
    grad_b = call(adapter_kernel, sds((rank, width), F32), *v_all, s_own)
    out = call(combine_kernel, sds(tokens.shape, BF), code, home)
    return out, grad_a[None], grad_b[None]


def solution(mesh):
    fine = Mesh(mesh.devices.reshape(4, 2, 4, 4, 4), ("x", "c", "zh", "zl", "y"))
    dp, ex = ("x", "c"), ("zh", "zl", "y")
    specs = (
        P(ex, dp), P(ex, dp), P(ex, None), P(ex, None),
        P(ex, dp, None), P(ex, dp, None), P(ex, dp, None), P(ex, None, dp), P(ex, None, dp),
    )
    return jax.shard_map(
        per_device,
        mesh=fine,
        in_specs=specs,
        out_specs=(P(ex, dp), P(ex, None, dp), P(ex, None, dp)),
        check_vma=False,
    )
```

```python
import jax
import jax.numpy as jnp
from jax import lax
from jax.experimental import pallas as pl
from jax.experimental.pallas import tpu as pltpu
from jax.sharding import Mesh, PartitionSpec as P

CAP = 5
BF = jnp.bfloat16
F32 = jnp.float32
LANE = 128
FLAT = 4
PARAMS = pltpu.CompilerParams(vmem_limit_bytes=16 * 1024 * 1024)


def nt(left, right):
    return lax.dot_general(left, right, (((1,), (1,)), ((), ())), preferred_element_type=F32)


def tn(left, right):
    return lax.dot_general(left, right, (((0,), (0,)), ((), ())), preferred_element_type=F32)


def nn(left, right):
    return jnp.dot(left, right, preferred_element_type=F32)


def lanes(index, width):
    return pl.ds(pl.multiple_of(index * width, width), width)


def fetch(pairs, sems):
    copies = [pltpu.make_async_copy(src, dst, sems.at[i]) for i, (src, dst) in enumerate(pairs)]
    for copy in copies:
        copy.start()
    for copy in copies:
        copy.wait()


def low(value, size):
    return value & (size - 1)


def high(value, size):
    return value >> (size.bit_length() - 1)


def expert_of(place):
    outer, inner = high(place, FLAT * FLAT), low(place, FLAT * FLAT)
    return low(inner, FLAT) * (FLAT * FLAT) + outer * FLAT + high(inner, FLAT)


def pack_kernel(ids_hbm, prob_hbm, tok_hbm, dy_hbm, out_ref, ids_ref, prob_ref, tok_ref, dy_ref, sems):
    fetch(
        [(ids_hbm, ids_ref), (prob_hbm, prob_ref), (tok_hbm, tok_ref), (dy_hbm, dy_ref)], sems
    )
    rows = out_ref.shape[0]
    count, width = tok_ref.shape
    parts = 2 * width // LANE
    span = parts * count
    row = lax.broadcasted_iota(jnp.int32, (rows, count), 0)
    own = expert_of(high(row, parts))
    hit = jnp.zeros((rows, count), F32)
    weight = jnp.zeros((rows, count), F32)
    for k in range(ids_ref.shape[0]):
        same = ids_ref[k : k + 1, :] == own
        hit = jnp.where(same, 1.0, hit)
        weight = jnp.where(same, prob_ref[k : k + 1, :], weight)
    weight = jnp.where(low(row, parts) < parts // 2, hit, weight)
    first = lax.broadcasted_iota(jnp.int32, (count, count), 0)
    second = lax.broadcasted_iota(jnp.int32, (count, count), 1)
    before = jnp.where(first < second, 1.0, 0.0).astype(BF)
    code = jnp.where(hit > 0.5, nn(hit.astype(BF), before), -1.0)
    wide_row = lax.broadcasted_iota(jnp.int32, (rows, span), 0)
    lane = lax.broadcasted_iota(jnp.int32, (rows, span), 1)
    here = low(wide_row, parts) == high(lane, count)
    spread = jnp.where(here, jnp.concatenate([code] * parts, axis=1), -1.0)
    table = jnp.concatenate(
        [ref[:, c : c + LANE] for ref in (tok_ref, dy_ref) for c in range(0, width, LANE)], axis=0
    )
    for s in range(CAP):
        pick = jnp.where(spread == float(s), 1.0, 0.0).astype(BF)
        scale = jnp.sum(jnp.where(code == float(s), weight, 0.0), axis=1, keepdims=True)
        out_ref[:, s * LANE : (s + 1) * LANE] = (nn(pick, table) * scale).astype(BF)


def code_of(ids, experts):
    count = ids.shape[1]
    own = expert_of(lax.broadcasted_iota(jnp.int32, (experts, count), 0))
    hit = jnp.zeros((experts, count), F32)
    for k in range(ids.shape[0]):
        hit = jnp.where(ids[k : k + 1, :] == own, 1.0, hit)
    first = lax.broadcasted_iota(jnp.int32, (count, count), 0)
    second = lax.broadcasted_iota(jnp.int32, (count, count), 1)
    before = jnp.where(first < second, 1.0, 0.0).astype(BF)
    return jnp.where(hit > 0.5, nn(hit.astype(BF), before), -1.0)


def unpack(in_hbm, in_ref, rows_ref, first_part, sem):
    load = pltpu.make_async_copy(in_hbm, in_ref, sem)
    load.start()
    total = in_ref.shape[0]
    width = rows_ref.shape[1]
    half = width // LANE
    parts = 2 * half
    experts = total // parts
    first = lax.broadcasted_iota(jnp.int32, (half * experts, total), 0)
    second = lax.broadcasted_iota(jnp.int32, (half * experts, total), 1)
    there = low(first, experts) * parts + high(first, experts) + first_part
    perm = jnp.where(second == there, 1.0, 0.0).astype(BF)
    load.wait()
    rows = nn(perm, in_ref[...]).astype(BF)
    for r in range(half):
        for s in range(CAP):
            rows_ref[s * experts : (s + 1) * experts, r * LANE : (r + 1) * LANE] = rows[
                r * experts : (r + 1) * experts, s * LANE : (s + 1) * LANE
            ]


def split_x_kernel(in_hbm, x_hbm, in_ref, x_ref, sems):
    unpack(in_hbm, in_ref, x_ref, 0, sems.at[0])
    fetch([(x_ref, x_hbm.at[x]) for x in range(x_hbm.shape[0])], sems)


def split_s_kernel(in_hbm, s_hbm, in_ref, s_ref, sems):
    unpack(in_hbm, in_ref, s_ref, s_ref.shape[1] // LANE, sems.at[0])
    fetch([(s_ref, s_hbm)], sems)


def prep_kernel(me_ref, wg_ref, wu_ref, wd_ref, own_ref, swap_ref, d0_ref, d1_ref, d2_ref, d3_ref):
    chip, core = me_ref[0], me_ref[1]
    chips, units, width = swap_ref.shape[1:]
    for d, ref in enumerate((d0_ref, d1_ref, d2_ref, d3_ref)):
        ref[...] = wd_ref[:, lanes(lax.rem(chip + d, chips), 2 * width)]
    for x in range(chips):
        for ref, which in ((own_ref, core), (swap_ref, 1 - core)):
            cols = lanes(2 * x + which, width)
            ref[0, x] = wg_ref[:, cols]
            ref[1, x] = wu_ref[:, cols]


def part_kernel(me_ref, *refs):
    chip, core = me_ref[0], me_ref[1]
    sources, out_hbm, held, out_ref, sems = refs[:8], refs[8], refs[9:17], refs[17], refs[18]
    fetch(list(zip(sources, held)), sems)
    s_ref, t_ref, b_ref, o_ref = held[:4]
    units, width = held[4].shape[0], s_ref.shape[1]
    chips = out_ref.shape[0]
    mine, other = s_ref[...], t_ref[...]
    low = (nt(mine, b_ref[...]) + nt(other, o_ref[...])).astype(BF)
    for d, ref in enumerate(held[4:]):
        w_mine, w_other = ref[:, lanes(core, width)], ref[:, lanes(1 - core, width)]
        to = lax.rem(chip + chips - d, chips)
        out_ref[to, :, :units] = (nt(mine, w_mine) + nt(other, w_other)).astype(BF)
        out_ref[to, :, units:] = low
    fetch([(out_ref, out_hbm)], sems)


def gate_kernel(x_ref, own_ref, half_ref, keep_hbm, send_ref, keep_ref, sem):
    chips, routes, width = x_ref.shape
    units = own_ref.shape[2]
    keep = [jnp.zeros((routes, units), F32)] * 2
    send = [jnp.zeros((routes, units), F32)] * 2
    for x in range(chips):
        for i in range(2):
            keep[i] = keep[i] + nt(x_ref[x], own_ref[i, x])
    for i in range(2):
        keep_ref[i] = keep[i]
    store = pltpu.make_async_copy(keep_ref, keep_hbm, sem.at[0])
    store.start()
    for x in range(chips):
        for i in range(2):
            send[i] = send[i] + nt(x_ref[x], half_ref[i, x])
    for i in range(2):
        send_ref[i] = send[i].astype(BF)
    store.wait()


def grad_kernel(keep_hbm, got_hbm, in_hbm, a_hbm, out_ref, ga_ref, keep_ref, got_ref, in_ref, a_ref, sems):
    pairs = [(in_hbm, in_ref), (a_hbm, a_ref), (keep_hbm, keep_ref), (got_hbm, got_ref)]
    copies = [pltpu.make_async_copy(p, q, sems.at[i]) for i, (p, q) in enumerate(pairs)]
    for copy in copies:
        copy.start()
    for copy in copies[:2]:
        copy.wait()
    units = keep_ref.shape[2]
    total = in_ref[0].astype(F32)
    for x in range(1, in_ref.shape[0]):
        total += in_ref[x].astype(F32)
    low_u = total[:, units:].astype(BF)
    grad = total[:, :units] + nn(low_u, a_ref[...])
    for copy in copies[2:]:
        copy.wait()
    gate = keep_ref[0] + got_ref[0].astype(F32)
    up = keep_ref[1] + got_ref[1].astype(F32)
    sigma = jax.nn.sigmoid(gate)
    active = gate * sigma
    hidden = (active * up).astype(BF)
    ga_ref[...] = tn(low_u, hidden)
    out_ref[:, :units] = (grad * up * sigma * (1.0 + gate * (1.0 - sigma))).astype(BF)
    low_v = nt(hidden, a_ref[...]).astype(BF)
    out_ref[:, units:] = jnp.concatenate([(grad * active).astype(BF), low_v], axis=1)


def back_kernel(g_ref, h_ref, own_ref, half_ref, out_hbm, v_ref, out_ref, out_sems):
    chips = out_ref.shape[0]
    units = own_ref.shape[2]
    mine = [g_ref[:, i * units : (i + 1) * units] for i in range(2)]
    other = [h_ref[:, i * units : (i + 1) * units] for i in range(2)]
    stores = []
    for x in range(chips):
        term = nn(mine[0], own_ref[0, x]) + nn(mine[1], own_ref[1, x])
        term += nn(other[0], half_ref[0, x]) + nn(other[1], half_ref[1, x])
        out_ref[x] = term.astype(BF)
        stores.append(pltpu.make_async_copy(out_ref.at[x], out_hbm.at[x], out_sems.at[x]))
        stores[x].start()
    v_ref[...] = (g_ref[:, 2 * units :].astype(F32) + h_ref[:, 2 * units :].astype(F32)).astype(BF)
    for store in stores:
        store.wait()


def code_kernel(ids_ref, code_ref):
    code_ref[...] = code_of(ids_ref[...], code_ref.shape[0])


def total_kernel(in_ref, out_ref):
    experts = out_ref.shape[0]
    width = in_ref.shape[2]
    for s in range(CAP):
        rows = slice(s * experts, (s + 1) * experts)
        total = in_ref[0, rows].astype(F32)
        for x in range(1, in_ref.shape[0]):
            total += in_ref[x, rows].astype(F32)
        out_ref[:, s * width : (s + 1) * width] = total.astype(BF)


def adapter_kernel(v0_ref, v1_ref, v2_ref, v3_ref, s_ref, o_ref):
    low = v0_ref[...].astype(F32) + v1_ref[...].astype(F32)
    low += v2_ref[...].astype(F32) + v3_ref[...].astype(F32)
    o_ref[...] = tn(low.astype(BF), s_ref[...])


def combine_kernel(code_ref, r_ref, o_ref):
    width = o_ref.shape[1]
    total = jnp.zeros(o_ref.shape, F32)
    for s in range(CAP):
        pick = jnp.where(code_ref[...] == float(s), 1.0, 0.0).astype(BF)
        total += tn(pick, r_ref[:, s * width : (s + 1) * width])
    o_ref[...] = total.astype(BF)


def call(body, outs, *args, scalars=0, places=(), ends=(), scratch=()):
    vmem = pl.BlockSpec(memory_space=pltpu.VMEM)
    smem = pl.BlockSpec(memory_space=pltpu.SMEM)
    places = places or [vmem] * (len(args) - scalars)
    return pl.pallas_call(
        body,
        out_shape=outs,
        in_specs=[smem] * scalars + list(places),
        out_specs=ends or jax.tree.map(lambda _: vmem, outs),
        scratch_shapes=list(scratch),
        compiler_params=PARAMS,
    )(*args)


def per_device(tokens, grad_out, prob, ids, w_gate, w_up, w_down, adapter_a, adapter_b):
    experts = lax.axis_size(("zh", "zl", "y"))
    chips = lax.axis_size("x")
    count, width = tokens.shape
    rank = adapter_b.shape[1]
    units = w_gate.shape[1]
    routes = experts * CAP
    w_gate, w_up, w_down, adapter_a, adapter_b = (
        w_gate[0], w_up[0], w_down[0], adapter_a[0], adapter_b[0],
    )
    sds = jax.ShapeDtypeStruct
    me = jnp.stack([lax.axis_index("x"), lax.axis_index("c")]).astype(jnp.int32)

    def swap(block):
        return lax.ppermute(block, "c", [(0, 1), (1, 0)])

    def shift(block, by):
        return lax.ppermute(block, "x", [(i, (i + by) % chips) for i in range(chips)])

    def over_x(block):
        return lax.all_to_all(block, "x", 0, 0, tiled=True)

    def route(block):
        return lax.all_to_all(block, ("zl", "y", "zh"), 0, 0, tiled=True)

    parts = 2 * width // LANE
    slow = pl.BlockSpec(memory_space=pltpu.HBM)

    def pin(*arrays):
        return [pltpu.with_memory_space_constraint(x, pltpu.HBM) for x in arrays]

    near = pl.BlockSpec(memory_space=pltpu.VMEM)
    far = pl.BlockSpec(memory_space=pltpu.HBM)
    dma = pltpu.SemaphoreType.DMA

    packed = call(
        pack_kernel, sds((experts * parts, CAP * LANE), BF),
        *pin(ids.T, prob.T, tokens, grad_out),
        places=[slow] * 4,
        scratch=[
            pltpu.VMEM(ids.T.shape, ids.dtype), pltpu.VMEM(prob.T.shape, F32),
            pltpu.VMEM(tokens.shape, BF), pltpu.VMEM(tokens.shape, BF), dma((4,)),
        ],
    )
    arrived = route(packed.reshape(experts, parts, CAP * LANE))

    own_cols, half, *down = call(
        prep_kernel,
        (sds((2, chips, units, width), BF),) * 2 + (sds((units, 2 * width), BF),) * 4,
        me, w_gate, w_up, w_down, scalars=1,
    )
    half = swap(half)
    down = down[:1] + [shift(block, d + 1) for d, block in enumerate(down[1:])]
    b_other = swap(adapter_b)
    arrived, half, b_other, *down = lax.optimization_barrier((arrived, half, b_other, *down))

    whole = arrived.reshape(experts * parts, CAP * LANE)
    scratch = [pltpu.VMEM(whole.shape, BF), pltpu.VMEM((routes, width), BF), dma((chips,))]
    x_four = call(
        split_x_kernel, pltpu.HBM((chips, routes, width), BF), *pin(whole), places=[slow], ends=far,
        scratch=scratch,
    )
    s_own = call(
        split_s_kernel, pltpu.HBM((routes, width), BF), *pin(whole), places=[slow], ends=far,
        scratch=scratch,
    )
    x_all = over_x(x_four)
    s_other = swap(s_own)
    shares = (chips, routes, units + rank)
    sources = (s_own, s_other, adapter_b, b_other, *down)
    part = call(
        part_kernel, pltpu.HBM(shares, BF), me, *pin(*sources), scalars=1,
        places=[slow] * len(sources), ends=far,
        scratch=[pltpu.VMEM(x.shape, BF) for x in (*sources, sds(shares, BF))] + [dma((len(sources),))],
    )
    sums = over_x(part)
    keep, send = call(
        gate_kernel,
        (pltpu.HBM((2, routes, units), F32), sds((2, routes, units), BF)),
        x_all, own_cols, half, ends=(far, near),
        scratch=[pltpu.VMEM((2, routes, units), F32), dma((1,))],
    )
    got = swap(send)
    sources = (keep, got, sums, adapter_a)
    grads, grad_a = call(
        grad_kernel,
        (sds((routes, 2 * units + rank), BF), sds((rank, units), F32)),
        *pin(*sources), places=[slow] * 4,
        scratch=[pltpu.VMEM(x.shape, x.dtype) for x in sources] + [dma((4,))],
    )
    grads_other = swap(grads)
    back_shape = (chips, routes, width)
    back, v_pair = call(
        back_kernel, (pltpu.HBM(back_shape, BF), sds((routes, rank), BF)),
        grads, grads_other, own_cols, half, ends=(far, near),
        scratch=[pltpu.VMEM(back_shape, BF), dma((chips,))],
    )
    code = call(code_kernel, sds((experts, count), F32), ids.T)
    backs, code = lax.optimization_barrier((over_x(back), code))
    total = call(total_kernel, sds((experts, CAP * width), BF), backs)
    home = route(total.reshape(experts, 2, CAP * width // 2)).reshape(experts, CAP * width)

    v_all = [v_pair] + [shift(v_pair, d) for d in (1, 2, 3)]
    grad_b = call(adapter_kernel, sds((rank, width), F32), *v_all, s_own)
    out = call(combine_kernel, sds(tokens.shape, BF), code, home)
    return out, grad_a[None], grad_b[None]


def solution(mesh):
    fine = Mesh(mesh.devices.reshape(4, 2, 4, 4, 4), ("x", "c", "zh", "zl", "y"))
    dp, ex = ("x", "c"), ("zh", "zl", "y")
    specs = (
        P(ex, dp), P(ex, dp), P(ex, None), P(ex, None),
        P(ex, dp, None), P(ex, dp, None), P(ex, dp, None), P(ex, None, dp), P(ex, None, dp),
    )
    return jax.shard_map(
        per_device,
        mesh=fine,
        in_specs=specs,
        out_specs=(P(ex, dp), P(ex, None, dp), P(ex, None, dp)),
        check_vma=False,
    )
```
